32 devices in a mesh: wide: 16 (over z, y, core), grp: 2 (over x).
Axes of the slice: x: 2, y: 2, z: 4, core: 2. Of those that a mesh axis runs over, the one named last changes fastest.
Arguments:
- tokens: bfloat16 [65536, 128], P(('grp', 'wide')), parts along dimension 0, may hold values from -6 to 6
- cotangent: bfloat16 [65536, 128], P(('grp', 'wide')), parts along dimension 0, may hold values from -6 to 6
- order_send: int32 [65536], P(('grp', 'wide')), parts along dimension 0, may hold values from 0 to 2047, as said below
- order_recv: int32 [65536], P(('grp', 'wide')), parts along dimension 0, may hold values from 0 to 2047, as said below
- gain_a: float32 [128], replicated, may hold values from 0.1 to 1.9
- qkv_a: bfloat16 [128, 384], replicated, may hold values from -0.35355339 to 0.35355339
- proj_a: bfloat16 [128, 128], replicated, may hold values from -0.5 to 0.5
- gain_b: float32 [128], replicated, may hold values from 0.1 to 1.9
- qkv_b: bfloat16 [128, 384], replicated, may hold values from -0.35355339 to 0.35355339
- proj_b: bfloat16 [128, 128], replicated, may hold values from -0.5 to 0.5
Outputs:
- d_tokens: bfloat16 [65536, 128], P(('grp', 'wide')), parts along dimension 0
- d_gain_a: float32 [256], P('grp'), parts along dimension 0
- d_qkv_a: float32 [256, 384], P('grp'), parts along dimension 0
- d_proj_a: float32 [256, 128], P('grp'), parts along dimension 0
- d_gain_b: float32 [256], P('grp'), parts along dimension 0
- d_qkv_b: float32 [256, 384], P('grp'), parts along dimension 0
- d_proj_b: float32 [256, 128], P('grp'), parts along dimension 0
The draws below stay inside these ranges and needn't reach their ends.
There are 2 independent parts, one for each index of `grp`. The reference program is written for one: setup_inputs(seed, part) draws one part's arguments, and reference() takes and returns one part's arrays. A program takes and returns all parts, laid end to end along the dimension named above; an argument that names none is the same for every part. Nothing has to cross between parts.
Inputs may be any that keep to these rules, and one draw needn't show every extreme that they name: Within every block of 2048 entries, order_send is a permutation of 0 to 2047. Within every block of 2048 entries, order_recv is a permutation of 0 to 2047.
All inputs are finite; a program needn't handle non-finite values.
Results may differ from the reference program's by a relative error of at most 0.03.
Values may be sent and summed in bfloat16 or wider, within the bound.
No kernel may reach another device: no remote copies, remote signals or barrier semaphores. Data moves between devices by JAX's collectives and lax.ppermute only.
A program may use at most 192 MiB of HBM per device.

```python
import jax
import jax.numpy as jnp
from jax import lax

D = 128
HEADS = 8
BALL = 256
ROWS_DEV = 2048
HEAD_DIM = 16
TOKENS = 32768
N_WIDE = 16


def local_orders(key):
    keys = jax.random.split(key, N_WIDE)
    return jax.vmap(lambda single: jax.random.permutation(single, ROWS_DEV))(keys).reshape(-1).astype(jnp.int32)


def draw_order_send(key, part):
    key = jax.random.fold_in(key, 11)
    return local_orders(key)


def draw_order_recv(key, part):
    key = jax.random.fold_in(key, 23)
    return local_orders(key)


def draw_tokens(key, part):
    key = jax.random.fold_in(key, 5)
    noise_key = jax.random.fold_in(key, 0)
    values = jax.random.normal(noise_key, (TOKENS, D), jnp.float32)
    return jnp.clip(values, -6.0, 6.0).astype(jnp.bfloat16)


def draw_qkv_a(key, part):
    key = jax.random.fold_in(key, 31)
    base_key = jax.random.fold_in(key, 0)
    limit = 4.0 * D ** (-0.5)
    values = jax.random.normal(base_key, (D, 3 * D), jnp.float32) * D ** (-0.5)
    return jnp.clip(values, -limit, limit).astype(jnp.bfloat16)


def draw_qkv_b(key, part):
    key = jax.random.fold_in(key, 37)
    base_key = jax.random.fold_in(key, 0)
    limit = 4.0 * D ** (-0.5)
    values = jax.random.normal(base_key, (D, 3 * D), jnp.float32) * D ** (-0.5)
    return jnp.clip(values, -limit, limit).astype(jnp.bfloat16)


def block_levels(own_key, extent, cuts, least, largest):
    level = 1.0
    for position, parts in cuts:
        draws = jax.random.uniform(jax.random.fold_in(jax.random.fold_in(own_key, 6), position), (parts,), jnp.float32, least / len(cuts), largest / len(cuts))
        level = level * jnp.repeat(jnp.exp(draws), extent[position] // parts).reshape((-1,) + (1,) * (len(extent) - 1 - position))
    return level


def scatter_about(own_key, dims, spread, most, cuts=(), kind=jnp.bfloat16):
    factor_of = block_levels(own_key, dims, cuts, -0.22, 0.18) if cuts else 1.0
    values = jax.random.normal(own_key, dims, jnp.float32) * spread * factor_of
    return jnp.minimum(jnp.maximum(values, -most), most).astype(kind)


def setup_inputs(seed: int = 0, part: int = 0) -> dict:
    streams_of = jax.random.split(jax.random.key(seed), 11)
    own_keys = jax.random.split(jax.random.fold_in(streams_of[10], part), 11)
    return {
        "tokens": draw_tokens(jax.random.fold_in(jax.random.fold_in(streams_of[10], part), 71), part),
        "cotangent": scatter_about(own_keys[1], (TOKENS, D), 1.0, 6.0, ((0, 16),)),
        "order_send": draw_order_send(jax.random.fold_in(jax.random.fold_in(streams_of[10], part), 71), part),
        "order_recv": draw_order_recv(jax.random.fold_in(jax.random.fold_in(streams_of[10], part), 71), part),
        "gain_a": jnp.clip(1.0 + 0.18 * jax.random.normal(streams_of[4], (D,), jnp.float32), 0.1, 1.9),
        "qkv_a": draw_qkv_a(jax.random.fold_in(streams_of[10], 71), part),
        "proj_a": scatter_about(streams_of[6], (D, D), D ** -0.5, 0.5),
        "gain_b": jnp.clip(1.0 + 0.18 * jax.random.normal(streams_of[7], (D,), jnp.float32), 0.1, 1.9),
        "qkv_b": draw_qkv_b(jax.random.fold_in(streams_of[10], 71), part),
        "proj_b": scatter_about(streams_of[9], (D, D), D ** -0.5, 0.5),
    }


def norm_rows(values, gain):
    mean_sq = lax.optimization_barrier(jnp.mean(values * values, axis=-1, keepdims=True))
    return values * lax.rsqrt(mean_sq + 1e-06) * gain

def ball_core(qkv):
    rows = qkv.shape[0]
    balls = qkv.astype(jnp.float32).reshape(rows // BALL, BALL, 3, HEADS, HEAD_DIM)
    query = balls[:, :, 0]
    keys = balls[:, :, 1]
    values = balls[:, :, 2]
    scores = jnp.einsum('bqhd,bkhd->bhqk', query, keys) * HEAD_DIM ** (-0.5)
    weights = jax.nn.softmax(scores, axis=-1).astype(jnp.bfloat16)
    attended = jnp.einsum('bhqk,bkhd->bqhd', weights.astype(jnp.float32), values)
    return attended.reshape(rows, D)

def mapped_core(qkv):
    grouped = qkv.reshape(N_WIDE, ROWS_DEV, 3 * D)
    return lax.map(ball_core, grouped).reshape(TOKENS, D)

def block_forward(rows_in, gain, w_qkv, w_proj):
    values = rows_in.astype(jnp.float32)
    normed = norm_rows(values, gain).astype(jnp.bfloat16)
    qkv = jnp.dot(normed, w_qkv, preferred_element_type=jnp.float32).astype(jnp.bfloat16)
    attended = mapped_core(qkv).astype(jnp.bfloat16)
    return (values + jnp.dot(attended, w_proj, preferred_element_type=jnp.float32)).astype(jnp.bfloat16)

def block_backward(rows_in, gain, w_qkv, w_proj, d_out):
    values = rows_in.astype(jnp.float32)
    normed_f, norm_back = jax.vjp(norm_rows, values, gain)
    normed = normed_f.astype(jnp.bfloat16)
    qkv = jnp.dot(normed, w_qkv, preferred_element_type=jnp.float32).astype(jnp.bfloat16)
    attended_f, core_back = jax.vjp(mapped_core, qkv)
    attended = attended_f.astype(jnp.bfloat16)
    d_proj = jnp.dot(attended.T, d_out, preferred_element_type=jnp.float32)
    d_att = jnp.dot(d_out, w_proj.T, preferred_element_type=jnp.float32).astype(jnp.bfloat16)
    d_rows_qkv = core_back(d_att.astype(jnp.float32))[0].astype(jnp.bfloat16)
    d_qkv = jnp.dot(normed.T, d_rows_qkv, preferred_element_type=jnp.float32)
    d_normed = jnp.dot(d_rows_qkv, w_qkv.T, preferred_element_type=jnp.float32)
    d_values, d_gain = norm_back(d_normed)
    d_in = (d_out.astype(jnp.float32) + d_values).astype(jnp.bfloat16)
    return (d_in, d_gain, d_qkv, d_proj)

def regroup(rows_in, order_send, order_recv):
    blocks = rows_in.reshape(N_WIDE, ROWS_DEV, D)
    sent = jnp.take_along_axis(blocks, order_send.reshape(N_WIDE, ROWS_DEV, 1).astype(jnp.int32), axis=1)
    pieces = sent.reshape(N_WIDE, N_WIDE, ROWS_DEV // N_WIDE, D).transpose(1, 0, 2, 3)
    received = pieces.reshape(N_WIDE, ROWS_DEV, D)
    placed = jnp.take_along_axis(received, order_recv.reshape(N_WIDE, ROWS_DEV, 1).astype(jnp.int32), axis=1)
    return placed.reshape(TOKENS, D)

def reference(tokens, cotangent, order_send, order_recv, gain_a, qkv_a, proj_a, gain_b, qkv_b, proj_b):
    first = block_forward(tokens, gain_a, qkv_a, proj_a)
    rotated, regroup_back = jax.vjp(lambda rows_in: regroup(rows_in, order_send, order_recv), first)
    d_rotated, d_gain_b, d_qkv_b, d_proj_b = block_backward(rotated, gain_b, qkv_b, proj_b, cotangent)
    d_first = regroup_back(d_rotated)[0]
    d_tokens, d_gain_a, d_qkv_a, d_proj_a = block_backward(tokens, gain_a, qkv_a, proj_a, d_first)
    return (d_tokens, d_gain_a, d_qkv_a, d_proj_a, d_gain_b, d_qkv_b, d_proj_b)
```

```python
import functools

import jax
import jax.numpy as jnp
from jax import lax
from jax.experimental import pallas as pl
from jax.experimental.pallas import tpu as pltpu
from jax.sharding import PartitionSpec as P

D = 128
HEADS = 8
BALL = 256
HEAD_DIM = 16
EPS = 1e-06
LOG2E = 1.4426950408889634
LN2 = 0.6931471805599453
SCALE = HEAD_DIM ** (-0.5)
VMEM_LIMIT = 56 * 1024 * 1024
UNROLL = 32
GRAD_ROWS = 4 * D + 32

f32 = jnp.float32
bf16 = jnp.bfloat16


def dot(a, b, ca=1, cb=0):
    return lax.dot_general(a, b, (((ca,), (cb,)), ((), ())), preferred_element_type=f32)


def head_mask(h):
    lane = lax.broadcasted_iota(jnp.int32, (1, D), 1)
    return jnp.where(lane // HEAD_DIM == h, 1.0, 0.0).astype(bf16)


def rows_of(h):
    return slice(h * HEAD_DIM, (h + 1) * HEAD_DIM)


def inverse_rms(values):
    return lax.rsqrt(jnp.mean(values * values, axis=-1, keepdims=True) + EPS)


def project(normed, w_ref, wt_ref):
    qkv_t = dot(wt_ref[...], normed, 1, 1)
    q_t = (qkv_t[:D] * (SCALE * LOG2E)).astype(bf16)
    k_t = qkv_t[D : 2 * D].astype(bf16)
    v_t = qkv_t[2 * D :].astype(bf16)
    kv = dot(normed, w_ref[:, D:]).astype(bf16)
    return q_t, k_t, v_t, kv[:, :D], kv[:, D:]


def forward_head(h, k_rows, q_t, v_t):
    scores = dot(k_rows * head_mask(h), q_t)
    top = jnp.max(scores, axis=0, keepdims=True)
    weights = jnp.exp2(scores - top).astype(bf16)
    ones = jnp.ones((HEAD_DIM, BALL), bf16)
    summed = dot(jnp.concatenate([v_t[rows_of(h)], ones], axis=0), weights)
    inv = 1.0 / summed[HEAD_DIM : HEAD_DIM + 1]
    return weights, inv, (summed[:HEAD_DIM] * inv).astype(bf16)


def backward_head(h, weights, att_t, d_att_t, q_t, k_t, v_rows, d_qkv_t_ref):
    rows = rows_of(h)
    own = d_att_t[rows]
    delta = jnp.sum(own.astype(f32) * att_t[rows].astype(f32), axis=0, keepdims=True)
    d_weights = dot(v_rows * head_mask(h), d_att_t)
    d_scores = (weights.astype(f32) * (d_weights - delta)).astype(bf16)
    d_qkv_t_ref[h * HEAD_DIM : (h + 1) * HEAD_DIM, :] = (dot(k_t[rows], d_scores) * SCALE).astype(bf16)
    d_qkv_t_ref[D + h * HEAD_DIM : D + (h + 1) * HEAD_DIM, :] = (dot(q_t[rows], d_scores, 1, 1) * LN2).astype(bf16)
    d_qkv_t_ref[2 * D + h * HEAD_DIM : 2 * D + (h + 1) * HEAD_DIM, :] = dot(own, weights, 1, 1).astype(bf16)


def backward_rows(values, inv_rms, gain, normed, w_ref, d_out, att_t, d_qkv_t, grads_ref):
    grads_ref[: 3 * D, :] += dot(d_qkv_t, normed)
    grads_ref[3 * D : 4 * D, :] += dot(att_t, d_out)
    d_normed = dot(w_ref[...], d_qkv_t).T
    unit = values * inv_rms
    grads_ref[4 * D : 4 * D + 1, :] += jnp.sum(d_normed * unit, axis=0, keepdims=True)
    d_unit = d_normed * gain
    along = jnp.mean(d_unit * unit, axis=-1, keepdims=True)
    return d_out.astype(f32) + inv_rms * (d_unit - unit * along)


def for_rows(count, copy_row):
    def step(i, carry):
        for j in range(UNROLL):
            copy_row(i * UNROLL + j)
        return carry

    lax.fori_loop(0, count // UNROLL, step, 0)


def first_kernel(order_ref, x_ref, gain_ref, w_ref, proj_ref, sent_ref, e_ref, inv_ref, att_ref, q_ref, k_ref, v_ref, wt, out, picked):
    ball = pl.program_id(0)

    @pl.when(ball == 0)
    def _():
        wt[...] = w_ref[...].T

    values = x_ref[...].astype(f32)
    normed = (values * inverse_rms(values) * gain_ref[...]).astype(bf16)
    q_t, k_t, v_t, k_rows, v_rows = project(normed, w_ref, wt)
    q_ref[0] = q_t
    k_ref[0] = k_t
    v_ref[...] = v_rows
    for h in range(HEADS):
        weights, inv, att = forward_head(h, k_rows, q_t, v_t)
        e_ref[0, h] = weights
        inv_ref[0, h : h + 1, :] = inv
        att_ref[0, rows_of(h), :] = att
    rows = values + dot(att_ref[0], proj_ref[...], 0, 0)
    out[pl.ds(pl.multiple_of(ball * BALL, BALL), BALL), :] = rows

    @pl.when(ball == pl.num_programs(0) - 1)
    def _():
        def pick(r):
            picked[pl.ds(r, 1), :] = out[pl.ds(order_ref[r], 1), :]

        for_rows(picked.shape[0], pick)
        sent_ref[...] = picked[...].astype(bf16)


def second_kernel(order_ref, came_ref, d_out_ref, gain_ref, w_ref, proj_ref, sent_ref, grads_ref, wt, came, placed, e_s, inv_s, att_s, d_qkv_t, d_in, d_came):
    ball = pl.program_id(0)

    @pl.when(ball == 0)
    def _():
        wt[...] = w_ref[...].T
        came[...] = came_ref[...].astype(f32)
        grads_ref[...] = jnp.zeros_like(grads_ref)

    base = ball * BALL

    def pick(r):
        placed[pl.ds(r, 1), :] = came[pl.ds(order_ref[base + r], 1), :]

    for_rows(BALL, pick)
    values = placed[...]
    inv_rms = inverse_rms(values)
    gain = gain_ref[...]
    normed = (values * inv_rms * gain).astype(bf16)
    q_t, k_t, v_t, k_rows, v_rows = project(normed, w_ref, wt)
    for h in range(HEADS):
        weights, inv, att = forward_head(h, k_rows, q_t, v_t)
        e_s[h] = weights
        inv_s[rows_of(h), :] = jnp.broadcast_to(inv, (HEAD_DIM, BALL))
        att_s[rows_of(h), :] = att
    d_out = d_out_ref[...]
    d_att_t = (dot(proj_ref[...], d_out, 1, 1) * inv_s[...]).astype(bf16)
    att_t = att_s[...]
    for h in range(HEADS):
        backward_head(h, e_s[h], att_t, d_att_t, q_t, k_t, v_rows, d_qkv_t)
    d_in[...] = backward_rows(values, inv_rms, gain, normed, w_ref, d_out, att_t, d_qkv_t[...], grads_ref)

    def put(r):
        d_came[pl.ds(order_ref[base + r], 1), :] = d_in[pl.ds(r, 1), :]

    for_rows(BALL, put)

    @pl.when(ball == pl.num_programs(0) - 1)
    def _():
        sent_ref[...] = d_came[...].astype(bf16)


def third_kernel(order_ref, came_ref, x_ref, gain_ref, w_ref, proj_ref, e_ref, inv_ref, att_ref, q_ref, k_ref, v_ref, d_x_ref, grads_ref, came, d_first, d_qkv_t):
    ball = pl.program_id(0)

    @pl.when(ball == 0)
    def _():
        came[...] = came_ref[...].astype(f32)
        grads_ref[...] = jnp.zeros_like(grads_ref)

        def put(r):
            d_first[pl.ds(order_ref[r], 1), :] = came[pl.ds(r, 1), :]

        for_rows(came.shape[0], put)

    values = x_ref[...].astype(f32)
    inv_rms = inverse_rms(values)
    gain = gain_ref[...]
    normed = (values * inv_rms * gain).astype(bf16)
    d_out = d_first[pl.ds(pl.multiple_of(ball * BALL, BALL), BALL), :].astype(bf16)
    d_att = dot(proj_ref[...], d_out, 1, 1)
    att_t, q_t, k_t, v_rows = att_ref[0], q_ref[0], k_ref[0], v_ref[...]
    d_att_t = jnp.concatenate([d_att[rows_of(h)] * inv_ref[0, h : h + 1, :] for h in range(HEADS)], axis=0).astype(bf16)
    for h in range(HEADS):
        backward_head(h, e_ref[0, h], att_t, d_att_t, q_t, k_t, v_rows, d_qkv_t)
    d_x = backward_rows(values, inv_rms, gain, normed, w_ref, d_out, att_t, d_qkv_t[...], grads_ref)
    d_x_ref[...] = d_x.astype(bf16)


def whole(shape):
    return pl.BlockSpec(shape, lambda i: (0,) * len(shape))


ORDER = pl.BlockSpec(memory_space=pltpu.SMEM)
BALL_ROWS = pl.BlockSpec((BALL, D), lambda i: (i, 0))
BALL_COLS = pl.BlockSpec((1, D, BALL), lambda i: (i, 0, 0))
BALL_STATS = pl.BlockSpec((1, HEADS, BALL), lambda i: (i, 0, 0))
BALL_WEIGHTS = pl.BlockSpec((1, HEADS, BALL, BALL), lambda i: (i, 0, 0, 0))
PARAMS = [whole((1, D)), whole((D, 3 * D)), whole((D, D))]


def call(kernel, grid, in_specs, outs, scratch):
    return pl.pallas_call(
        kernel,
        grid=(grid,),
        in_specs=in_specs,
        out_specs=[spec for spec, _, _ in outs],
        out_shape=[jax.ShapeDtypeStruct(shape, kind) for _, shape, kind in outs],
        scratch_shapes=[pltpu.VMEM(shape, kind) for shape, kind in scratch],
        compiler_params=pltpu.CompilerParams(vmem_limit_bytes=VMEM_LIMIT),
    )


def first_call(order, x, gain, w, proj):
    rows = x.shape[0]
    balls = rows // BALL
    return call(
        first_kernel,
        balls,
        [ORDER, BALL_ROWS] + PARAMS,
        [
            (whole((rows, D)), (rows, D), bf16),
            (BALL_WEIGHTS, (balls, HEADS, BALL, BALL), bf16),
            (BALL_STATS, (balls, HEADS, BALL), f32),
            (BALL_COLS, (balls, D, BALL), bf16),
            (BALL_COLS, (balls, D, BALL), bf16),
            (BALL_COLS, (balls, D, BALL), bf16),
            (BALL_ROWS, (rows, D), bf16),
        ],
        [((3 * D, D), bf16), ((rows, D), f32), ((rows, D), f32)],
    )(order, x, gain, w, proj)


def second_call(order, came, d_out, gain, w, proj):
    rows = came.shape[0]
    return call(
        second_kernel,
        rows // BALL,
        [ORDER, whole((rows, D)), BALL_ROWS] + PARAMS,
        [(whole((rows, D)), (rows, D), bf16), (whole((GRAD_ROWS, D)), (GRAD_ROWS, D), f32)],
        [
            ((3 * D, D), bf16),
            ((rows, D), f32),
            ((BALL, D), f32),
            ((HEADS, BALL, BALL), bf16),
            ((D, BALL), f32),
            ((D, BALL), bf16),
            ((3 * D, BALL), bf16),
            ((BALL, D), f32),
            ((rows, D), f32),
        ],
    )(order, came, d_out, gain, w, proj)


def third_call(order, came, x, gain, w, proj, kept):
    rows = came.shape[0]
    return call(
        third_kernel,
        rows // BALL,
        [ORDER, whole((rows, D)), BALL_ROWS] + PARAMS + [BALL_WEIGHTS, BALL_STATS, BALL_COLS, BALL_COLS, BALL_COLS, BALL_ROWS],
        [(BALL_ROWS, (rows, D), bf16), (whole((GRAD_ROWS, D)), (GRAD_ROWS, D), f32)],
        [((rows, D), f32), ((rows, D), f32), ((3 * D, BALL), bf16)],
    )(order, came, x, gain, w, proj, *kept)


def exchange(rows):
    return lax.all_to_all(rows, "wide", split_axis=0, concat_axis=0, tiled=True)


def swap(part, peers, apart):
    return lax.ppermute(part, "wide", [(i, i ^ apart) for i in range(peers)])


def sum_over_wide(part):
    peers = lax.axis_size("wide")
    half = part.shape[0] // 2
    core = lax.axis_index("wide") % 2
    part = part.astype(bf16)
    low, high = part[:half], part[half:]
    mine = jnp.where(core == 0, low, high)
    other = jnp.where(core == 0, high, low)
    total = mine.astype(f32) + swap(other, peers, 1).astype(f32)
    apart = 2
    while apart < peers:
        sent = total.astype(bf16)
        total = sent.astype(f32) + swap(sent, peers, apart).astype(f32)
        apart *= 2
    mine = total.astype(bf16)
    other = swap(mine, peers, 1)
    low = jnp.where(core == 0, mine, other)
    high = jnp.where(core == 0, other, mine)
    return jnp.concatenate([low, high], axis=0).astype(f32)


def body(tokens, cotangent, order_send, order_recv, gain_a, qkv_a, proj_a, gain_b, qkv_b, proj_b):
    gain_a = gain_a.reshape(1, D)
    gain_b = gain_b.reshape(1, D)
    sent, *kept = first_call(order_send, tokens, gain_a, qkv_a, proj_a)
    d_sent, grads_b = second_call(order_recv, exchange(sent), cotangent, gain_b, qkv_b, proj_b)
    d_tokens, grads_a = third_call(order_send, exchange(d_sent), tokens, gain_a, qkv_a, proj_a, kept)
    total = sum_over_wide(jnp.concatenate([grads_a, grads_b], axis=0))
    outs = [d_tokens]
    for start in (0, GRAD_ROWS):
        outs.append(total[start + 4 * D])
        outs.append(total[start : start + 3 * D].T)
        outs.append(total[start + 3 * D : start + 4 * D])
    return tuple(outs)


def solution(mesh):
    rows = P(("grp", "wide"), None)
    order = P(("grp", "wide"))
    return jax.shard_map(
        body,
        mesh=mesh,
        in_specs=(rows, rows, order, order) + (P(),) * 6,
        out_specs=(rows,) + (P("grp"), P("grp", None), P("grp", None)) * 2,
        check_vma=False,
    )
```

```python
import jax
import jax.numpy as jnp
from jax import lax
from jax.experimental import pallas as pl
from jax.experimental.pallas import tpu as pltpu
from jax.sharding import PartitionSpec as P

D = 128
HEADS = 8
BALL = 256
HEAD_DIM = 16
EPS = 1e-06
LOG2E = 1.4426950408889634
LN2 = 0.6931471805599453
SCALE = HEAD_DIM ** (-0.5)
VMEM_LIMIT = 56 * 1024 * 1024
CHUNK = BALL // HEADS
GRAD_HALF = 2 * D + 16

f32 = jnp.float32
bf16 = jnp.bfloat16


def dot(a, b, ca=1, cb=0):
    return lax.dot_general(a, b, (((ca,), (cb,)), ((), ())), preferred_element_type=f32)


def head_mask(h):
    lane = lax.broadcasted_iota(jnp.int32, (1, D), 1)
    return jnp.where(lane // HEAD_DIM == h, 1.0, 0.0).astype(bf16)


def rows_of(h):
    return slice(h * HEAD_DIM, (h + 1) * HEAD_DIM)


def inverse_rms(values):
    return lax.rsqrt(jnp.mean(values * values, axis=-1, keepdims=True) + EPS)


def staggered(count, *stages):
    last = max(lag for lag, _ in stages)
    for step in range(count + last):
        for lag, stage in stages:
            if 0 <= step - lag < count:
                stage(step - lag)


def at_first(stage):
    return lambda i: stage(i // HEADS) if i % HEADS == 0 else None


def at_last(stage):
    return lambda i: stage(i // HEADS) if i % HEADS == HEADS - 1 else None


def ball_rows(ball):
    return slice(ball * BALL, (ball + 1) * BALL)


def project(normed, w_ref, wt_ref):
    qkv_t = dot(wt_ref[...], normed, 1, 1)
    q_t = (qkv_t[:D] * (SCALE * LOG2E)).astype(bf16)
    k_t = qkv_t[D : 2 * D].astype(bf16)
    v_t = qkv_t[2 * D :].astype(bf16)
    kv = dot(normed, w_ref[:, D:]).astype(bf16)
    return q_t, k_t, v_t, kv[:, :D], kv[:, D:]


class Forward:
    def __init__(self, e_ref, inv_ref, att_ref):
        self.e_ref, self.inv_ref, self.att_ref = e_ref, inv_ref, att_ref
        self.parts, self.scores = {}, {}

    def score(self, i):
        ball, h = divmod(i, HEADS)
        q_t, _, _, k_rows, _ = self.parts[ball]
        self.scores[i] = dot(k_rows * head_mask(h), q_t)

    def soften(self, i):
        ball, h = divmod(i, HEADS)
        own = self.scores.pop(i)
        self.e_ref[ball, h] = jnp.exp2(own - jnp.max(own, axis=0, keepdims=True)).astype(bf16)

    def attend(self, i):
        ball, h = divmod(i, HEADS)
        ones = jnp.ones((HEAD_DIM, BALL), bf16)
        stacked = jnp.concatenate([self.parts[ball][2][rows_of(h)], ones], axis=0)
        summed = dot(stacked, self.e_ref[ball, h])
        inv = 1.0 / summed[HEAD_DIM : HEAD_DIM + 1]
        self.inv_ref[ball, h : h + 1, :] = inv
        self.att_ref[ball, rows_of(h), :] = (summed[:HEAD_DIM] * inv).astype(bf16)


class Backward:
    def __init__(self, e_ref, inv_ref, att_ref, d_s, d_qkv_t, w_ref, proj_ref, gain_ref, sums):
        self.e_ref, self.inv_ref, self.att_ref, self.d_s, self.d_qkv_t = e_ref, inv_ref, att_ref, d_s, d_qkv_t
        self.w_ref, self.proj_ref, self.gain_ref, self.sums = w_ref, proj_ref, gain_ref, sums
        self.parts, self.rows, self.d_out, self.d_att, self.d_weights = {}, {}, {}, {}, {}

    def join(self, ball, d_out):
        inv = [jnp.broadcast_to(self.inv_ref[ball, h : h + 1, :], (HEAD_DIM, BALL)) for h in range(HEADS)]
        self.d_out[ball] = d_out
        self.d_att[ball] = (dot(self.proj_ref[...], d_out, 1, 1) * jnp.concatenate(inv, axis=0)).astype(bf16)

    def weigh(self, i):
        ball, h = divmod(i, HEADS)
        self.d_weights[i] = dot(self.parts[ball][2] * head_mask(h), self.d_att[ball])

    def score(self, i):
        ball, h = divmod(i, HEADS)
        own = self.d_att[ball][rows_of(h)]
        att = self.att_ref[ball, rows_of(h), :]
        delta = jnp.sum(own.astype(f32) * att.astype(f32), axis=0, keepdims=True)
        self.d_s[ball, h] = (self.e_ref[ball, h].astype(f32) * (self.d_weights.pop(i) - delta)).astype(bf16)

    def put(self, part, ball, h, value):
        start = part * D + h * HEAD_DIM
        self.d_qkv_t[ball, start : start + HEAD_DIM, :] = value.astype(bf16)

    def value(self, i):
        ball, h = divmod(i, HEADS)
        self.put(2, ball, h, dot(self.d_att[ball][rows_of(h)], self.e_ref[ball, h], 1, 1))

    def query_key(self, i):
        ball, h = divmod(i, HEADS)
        q_t, k_t, _ = self.parts[ball]
        self.put(0, ball, h, dot(k_t[rows_of(h)], self.d_s[ball, h]) * SCALE)
        self.put(1, ball, h, dot(q_t[rows_of(h)], self.d_s[ball, h], 1, 1) * LN2)

    def finish(self, ball):
        values, inv_rms, normed = self.rows.pop(ball)
        d_out, d_qkv_t = self.d_out.pop(ball), self.d_qkv_t[ball]
        self.sums[: 3 * D, :] += dot(d_qkv_t, normed)
        self.sums[3 * D : 4 * D, :] += dot(self.att_ref[ball], d_out)
        d_normed = dot(self.w_ref[...], d_qkv_t).T
        unit = values * inv_rms
        self.sums[4 * D : 4 * D + 1, :] += jnp.sum(d_normed * unit, axis=0, keepdims=True)
        d_unit = d_normed * self.gain_ref[...]
        along = jnp.mean(d_unit * unit, axis=-1, keepdims=True)
        return d_out.astype(f32) + inv_rms * (d_unit - unit * along)


def normalise(values, gain_ref):
    inv_rms = inverse_rms(values)
    return inv_rms, (values * inv_rms * gain_ref[...]).astype(bf16)


def gather(rows, order_ref, from_ref, to_ref):
    for r in rows:
        to_ref[pl.ds(r, 1), :] = from_ref[pl.ds(order_ref[r], 1), :]


def scatter(rows, order_ref, from_ref, to_ref):
    for r in rows:
        to_ref[pl.ds(order_ref[r], 1), :] = from_ref[pl.ds(r, 1), :]


def chunk(i):
    return range(i * CHUNK, (i + 1) * CHUNK)


def arranged(sums):
    gain = sums[4 * D : 4 * D + 16, :]
    parts = [sums[0:D, :].T, sums[D : 2 * D, :].T, gain, sums[2 * D : 3 * D, :].T, sums[3 * D : 4 * D, :], gain]
    return jnp.concatenate(parts, axis=0)


def first_kernel(order_ref, x_ref, gain_ref, w_ref, proj_ref, sent_ref, inverse_ref, inv_ref, e_out, kept_out, v_out, wt, out, sent, e_s, kept, v_s, att_s, sems):
    balls = e_s.shape[0]
    heads = balls * HEADS
    wt[...] = w_ref[...].T
    forward = Forward(e_s, inv_ref, att_s)
    values, copies = {}, []

    def invert(i):
        for r in chunk(i):
            inverse_ref[order_ref[r]] = r

    def prepare(ball):
        values[ball] = x_ref[ball_rows(ball), :].astype(f32)
        _, normed = normalise(values[ball], gain_ref)
        parts = project(normed, w_ref, wt)
        forward.parts[ball] = parts
        kept[ball, D : 2 * D, :] = parts[0]
        kept[ball, 2 * D :, :] = parts[1]
        v_s[ball] = parts[4]

    def finish(ball):
        att_t = att_s[ball]
        kept[ball, :D, :] = att_t
        out[ball_rows(ball), :] = values.pop(ball) + dot(att_t, proj_ref[...], 0, 0)
        for n, (source, target) in enumerate(((e_s, e_out), (kept, kept_out), (v_s, v_out))):
            copy = pltpu.make_async_copy(source.at[ball], target.at[ball], sems.at[n, ball])
            copy.start()
            copies.append(copy)

    early = 2 * HEADS

    def invert_early(i):
        if i < early:
            for n in range(i * heads // early, (i + 1) * heads // early):
                invert(n)

    staggered(
        heads,
        (0, at_first(prepare)),
        (0, invert_early),
        (2, forward.score),
        (6, forward.soften),
        (8, forward.attend),
        (8, at_last(finish)),
        (17, lambda i: scatter(chunk(i), inverse_ref, out, sent)),
    )
    sent_ref[...] = sent[...].astype(bf16)
    for copy in copies:
        copy.wait()


def second_kernel(order_ref, came_ref, d_out_ref, gain_ref, w_ref, proj_ref, sent_ref, grads_ref, wt, came, placed, e_s, inv_s, att_s, d_s, d_qkv_t, d_in, d_came, sums):
    balls = e_s.shape[0]
    wt[...] = w_ref[...].T
    came[...] = came_ref[...].astype(f32)
    sums[...] = jnp.zeros_like(sums)
    forward = Forward(e_s, inv_s, att_s)
    backward = Backward(e_s, inv_s, att_s, d_s, d_qkv_t, w_ref, proj_ref, gain_ref, sums)

    def prepare(ball):
        values = placed[ball_rows(ball), :]
        inv_rms, normed = normalise(values, gain_ref)
        parts = project(normed, w_ref, wt)
        forward.parts[ball] = parts
        backward.parts[ball] = (parts[0], parts[1], parts[4])
        backward.rows[ball] = (values, inv_rms, normed)

    def join(ball):
        backward.join(ball, d_out_ref[ball_rows(ball), :])

    def finish(ball):
        d_in[ball_rows(ball), :] = backward.finish(ball)

    staggered(
        balls * HEADS,
        (0, lambda i: gather(chunk(i), order_ref, came, placed)),
        (8, at_first(prepare)),
        (10, forward.score),
        (14, forward.soften),
        (16, forward.attend),
        (16, at_last(join)),
        (25, backward.weigh),
        (28, backward.score),
        (28, backward.value),
        (30, backward.query_key),
        (30, at_last(finish)),
        (39, lambda i: scatter(chunk(i), order_ref, d_in, d_came)),
    )
    sent_ref[...] = d_came[...].astype(bf16)
    grads_ref[...] = arranged(sums)


def third_kernel(core_ref, inverse_ref, came_ref, x_ref, gain_ref, w_ref, proj_ref, inv_ref, other_ref, e_in, kept_in, v_in, d_x_ref, mine_ref, sent_ref, came, d_first, e_s, kept, v_s, d_s, d_qkv_t, sums, halves, sems):
    balls = e_s.shape[0]
    copies = {}
    for ball in range(balls):
        for n, (source, target) in enumerate(((e_in, e_s), (kept_in, kept), (v_in, v_s))):
            copies[ball, n] = pltpu.make_async_copy(source.at[ball], target.at[ball], sems.at[n, ball])
            copies[ball, n].start()
    came[...] = came_ref[...].astype(f32)
    sums[...] = jnp.zeros_like(sums)
    backward = Backward(e_s, inv_ref, kept.at[:, :D, :], d_s, d_qkv_t, w_ref, proj_ref, gain_ref, sums)

    def prepare(ball):
        for n in range(3):
            copies[ball, n].wait()
        values = x_ref[ball_rows(ball), :].astype(f32)
        inv_rms, normed = normalise(values, gain_ref)
        backward.rows[ball] = (values, inv_rms, normed)
        backward.parts[ball] = (kept[ball, D : 2 * D, :], kept[ball, 2 * D :, :], v_s[ball])
        backward.join(ball, d_first[ball_rows(ball), :].astype(bf16))

    def finish(ball):
        d_x_ref[ball_rows(ball), :] = backward.finish(ball).astype(bf16)

    staggered(
        balls * HEADS,
        (0, lambda i: gather(chunk(i), inverse_ref, came, d_first)),
        (8, at_first(prepare)),
        (10, backward.weigh),
        (13, backward.score),
        (13, backward.value),
        (15, backward.query_key),
        (15, at_last(finish)),
    )
    halves[...] = arranged(sums)
    core = core_ref[0]
    for n, ref in enumerate((halves, other_ref)):
        block = slice(n * GRAD_HALF, (n + 1) * GRAD_HALF)
        mine_ref[block, :] = ref[pl.ds(pl.multiple_of(core * GRAD_HALF, 16), GRAD_HALF), :]
        sent_ref[block, :] = ref[pl.ds(pl.multiple_of((1 - core) * GRAD_HALF, 16), GRAD_HALF), :].astype(bf16)


def last_kernel(core_ref, mine_ref, came_ref, *out_refs):
    first = core_ref[0] == 0
    mine, came = mine_ref[...].astype(f32), came_ref[...].astype(f32)
    low = jnp.where(first, mine, came)
    high = jnp.where(first, came, mine)
    for n in range(2):
        gain_ref, qkv_ref, proj_ref = out_refs[3 * n : 3 * n + 3]
        start = n * GRAD_HALF
        qkv_ref[:, :D] = low[start : start + D]
        qkv_ref[:, D : 2 * D] = low[start + D : start + 2 * D]
        gain_ref[...] = low[start + 2 * D : start + 2 * D + 1]
        qkv_ref[:, 2 * D :] = high[start : start + D]
        proj_ref[...] = high[start + D : start + 2 * D]


SCALARS = pl.BlockSpec(memory_space=pltpu.SMEM)
VECTORS = pl.BlockSpec(memory_space=pltpu.VMEM)
REMAIN = pl.BlockSpec(memory_space=pl.ANY)


def call(kernel, in_specs, outs, scratch):
    return pl.pallas_call(
        kernel,
        in_specs=in_specs,
        out_specs=[spec for spec, _, _ in outs],
        out_shape=[jax.ShapeDtypeStruct(shape, kind) for _, shape, kind in outs],
        scratch_shapes=scratch,
        compiler_params=pltpu.CompilerParams(vmem_limit_bytes=VMEM_LIMIT),
    )


def first_call(order, x, gain, w, proj):
    rows = x.shape[0]
    balls = rows // BALL
    kept = [((balls, HEADS, BALL, BALL), bf16), ((balls, 3 * D, BALL), bf16), ((balls, BALL, D), bf16)]
    return call(
        first_kernel,
        [SCALARS] + [VECTORS] * 4,
        [(VECTORS, (rows, D), bf16), (SCALARS, (rows,), jnp.int32), (VECTORS, (balls, HEADS, BALL), f32)]
        + [(REMAIN, shape, kind) for shape, kind in kept],
        [pltpu.VMEM((3 * D, D), bf16), pltpu.VMEM((rows, D), f32), pltpu.VMEM((rows, D), f32)]
        + [pltpu.VMEM(shape, kind) for shape, kind in kept]
        + [pltpu.VMEM((balls, D, BALL), bf16), pltpu.SemaphoreType.DMA((3, balls))],
    )(order, x, gain, w, proj)


def second_call(order, came, d_out, gain, w, proj):
    rows = came.shape[0]
    balls = rows // BALL
    weights = pltpu.VMEM((balls, HEADS, BALL, BALL), bf16)
    return call(
        second_kernel,
        [SCALARS] + [VECTORS] * 5,
        [(VECTORS, (rows, D), bf16), (VECTORS, (2 * GRAD_HALF, D), f32)],
        [
            pltpu.VMEM((3 * D, D), bf16),
            pltpu.VMEM((rows, D), f32),
            pltpu.VMEM((rows, D), f32),
            weights,
            pltpu.VMEM((balls, HEADS, BALL), f32),
            pltpu.VMEM((balls, D, BALL), bf16),
            weights,
            pltpu.VMEM((balls, 3 * D, BALL), bf16),
            pltpu.VMEM((rows, D), f32),
            pltpu.VMEM((rows, D), f32),
            pltpu.VMEM((4 * D + 16, D), f32),
        ],
    )(order, came, d_out, gain, w, proj)


def third_call(core, inverse, came, x, gain, w, proj, inv, other, kept):
    rows = came.shape[0]
    balls = rows // BALL
    weights = pltpu.VMEM((balls, HEADS, BALL, BALL), bf16)
    return call(
        third_kernel,
        [SCALARS] * 2 + [VECTORS] * 7 + [REMAIN] * 3,
        [(VECTORS, (rows, D), bf16), (VECTORS, (2 * GRAD_HALF, D), f32), (VECTORS, (2 * GRAD_HALF, D), bf16)],
        [pltpu.VMEM((rows, D), f32), pltpu.VMEM((rows, D), f32)]
        + [pltpu.VMEM(part.shape, part.dtype) for part in kept]
        + [
            weights,
            pltpu.VMEM((balls, 3 * D, BALL), bf16),
            pltpu.VMEM((4 * D + 16, D), f32),
            pltpu.VMEM((2 * GRAD_HALF, D), f32),
            pltpu.SemaphoreType.DMA((3, balls)),
        ],
    )(core, inverse, came, x, gain, w, proj, inv, other, *kept)


def last_call(core, mine, came):
    shapes = [(1, D), (D, 3 * D), (D, D)] * 2
    return call(last_kernel, [SCALARS] + [VECTORS] * 2, [(VECTORS, shape, f32) for shape in shapes], [])(core, mine, came)


def exchange(rows):
    return lax.all_to_all(rows, "wide", split_axis=0, concat_axis=0, tiled=True)


def swap(part, peers, apart):
    return lax.ppermute(part, "wide", [(i, i ^ apart) for i in range(peers)])


def body(tokens, cotangent, order_send, order_recv, gain_a, qkv_a, proj_a, gain_b, qkv_b, proj_b):
    peers = lax.axis_size("wide")
    core = (lax.axis_index("wide") % 2).astype(jnp.int32).reshape(1)
    gain_a = gain_a.reshape(1, D)
    gain_b = gain_b.reshape(1, D)
    sent, inverse, inv, *kept = first_call(order_send, tokens, gain_a, qkv_a, proj_a)
    d_sent, grads_b = second_call(order_recv, exchange(sent), cotangent, gain_b, qkv_b, proj_b)
    d_tokens, mine, other = third_call(
        core, inverse, exchange(d_sent), tokens, gain_a, qkv_a, proj_a, inv, grads_b, kept
    )
    total = mine + swap(other, peers, 1).astype(f32)
    apart = 2
    while apart < peers:
        part = total.astype(bf16)
        total = part.astype(f32) + swap(part, peers, apart).astype(f32)
        apart *= 2
    part = total.astype(bf16)
    sums = last_call(core, part, swap(part, peers, 1))
    d_gain_a, d_qkv_a, d_proj_a, d_gain_b, d_qkv_b, d_proj_b = sums
    return d_tokens, d_gain_a.reshape(D), d_qkv_a, d_proj_a, d_gain_b.reshape(D), d_qkv_b, d_proj_b


def solution(mesh):
    rows = P(("grp", "wide"), None)
    order = P(("grp", "wide"))
    return jax.shard_map(
        body,
        mesh=mesh,
        in_specs=(rows, rows, order, order) + (P(),) * 6,
        out_specs=(rows,) + (P("grp"), P("grp", None), P("grp", None)) * 2,
        check_vma=False,
    )
```

```python
import jax
import jax.numpy as jnp
from jax import lax
from jax.experimental import pallas as pl
from jax.experimental.pallas import tpu as pltpu
from jax.sharding import PartitionSpec as P

D = 128
HEADS = 8
BALL = 256
HEAD_DIM = 16
EPS = 1e-06
LOG2E = 1.4426950408889634
LN2 = 0.6931471805599453
SCALE = HEAD_DIM ** (-0.5)
VMEM_LIMIT = 56 * 1024 * 1024
UNROLL = 32
AHEAD = 3
CHUNK = BALL // HEADS
GRAD_HALF = 2 * D + 16

f32 = jnp.float32
bf16 = jnp.bfloat16


def dot(a, b, ca=1, cb=0):
    return lax.dot_general(a, b, (((ca,), (cb,)), ((), ())), preferred_element_type=f32)


def head_mask(h):
    lane = lax.broadcasted_iota(jnp.int32, (1, D), 1)
    return jnp.where(lane // HEAD_DIM == h, 1.0, 0.0).astype(bf16)


def rows_of(h):
    return slice(h * HEAD_DIM, (h + 1) * HEAD_DIM)


def inverse_rms(values):
    return lax.rsqrt(jnp.mean(values * values, axis=-1, keepdims=True) + EPS)


def staggered(count, *stages):
    last = max(lag for lag, _ in stages)
    for step in range(count + last):
        for lag, stage in stages:
            if 0 <= step - lag < count:
                stage(step - lag)


def at_first(stage):
    return lambda i: stage(i // HEADS) if i % HEADS == 0 else None


def at_last(stage):
    return lambda i: stage(i // HEADS) if i % HEADS == HEADS - 1 else None


def ball_rows(ball):
    return slice(ball * BALL, (ball + 1) * BALL)


def project(normed, w_ref, wt_ref):
    qkv_t = dot(wt_ref[...], normed, 1, 1)
    q_t = (qkv_t[:D] * (SCALE * LOG2E)).astype(bf16)
    k_t = qkv_t[D : 2 * D].astype(bf16)
    v_t = qkv_t[2 * D :].astype(bf16)
    kv = dot(normed, w_ref[:, D:]).astype(bf16)
    return q_t, k_t, v_t, kv[:, :D], kv[:, D:]


class Forward:
    def __init__(self, e_ref, inv_ref, att_ref):
        self.e_ref, self.inv_ref, self.att_ref = e_ref, inv_ref, att_ref
        self.parts, self.scores = {}, {}

    def score(self, i):
        ball, h = divmod(i, HEADS)
        q_t, _, _, k_rows, _ = self.parts[ball]
        self.scores[i] = dot(k_rows * head_mask(h), q_t)

    def soften(self, i):
        ball, h = divmod(i, HEADS)
        own = self.scores.pop(i)
        self.e_ref[ball, h] = jnp.exp2(own - jnp.max(own, axis=0, keepdims=True)).astype(bf16)

    def attend(self, i):
        ball, h = divmod(i, HEADS)
        ones = jnp.ones((HEAD_DIM, BALL), bf16)
        stacked = jnp.concatenate([self.parts[ball][2][rows_of(h)], ones], axis=0)
        summed = dot(stacked, self.e_ref[ball, h])
        inv = 1.0 / summed[HEAD_DIM : HEAD_DIM + 1]
        self.inv_ref[ball, h : h + 1, :] = inv
        self.att_ref[ball, rows_of(h), :] = (summed[:HEAD_DIM] * inv).astype(bf16)


class Backward:
    def __init__(self, e_ref, inv_ref, att_ref, d_s, d_qkv_t, w_ref, proj_ref, gain_ref, sums):
        self.e_ref, self.inv_ref, self.att_ref, self.d_s, self.d_qkv_t = e_ref, inv_ref, att_ref, d_s, d_qkv_t
        self.w_ref, self.proj_ref, self.gain_ref, self.sums = w_ref, proj_ref, gain_ref, sums
        self.parts, self.rows, self.d_out, self.d_att, self.d_weights = {}, {}, {}, {}, {}

    def join(self, ball, d_out):
        inv = [jnp.broadcast_to(self.inv_ref[ball, h : h + 1, :], (HEAD_DIM, BALL)) for h in range(HEADS)]
        self.d_out[ball] = d_out
        self.d_att[ball] = (dot(self.proj_ref[...], d_out, 1, 1) * jnp.concatenate(inv, axis=0)).astype(bf16)

    def weigh(self, i):
        ball, h = divmod(i, HEADS)
        self.d_weights[i] = dot(self.parts[ball][2] * head_mask(h), self.d_att[ball])

    def score(self, i):
        ball, h = divmod(i, HEADS)
        own = self.d_att[ball][rows_of(h)]
        att = self.att_ref[ball, rows_of(h), :]
        delta = jnp.sum(own.astype(f32) * att.astype(f32), axis=0, keepdims=True)
        self.d_s[ball, h] = (self.e_ref[ball, h].astype(f32) * (self.d_weights.pop(i) - delta)).astype(bf16)

    def put(self, part, ball, h, value):
        start = part * D + h * HEAD_DIM
        self.d_qkv_t[ball, start : start + HEAD_DIM, :] = value.astype(bf16)

    def value(self, i):
        ball, h = divmod(i, HEADS)
        self.put(2, ball, h, dot(self.d_att[ball][rows_of(h)], self.e_ref[ball, h], 1, 1))

    def query_key(self, i):
        ball, h = divmod(i, HEADS)
        q_t, k_t, _ = self.parts[ball]
        self.put(0, ball, h, dot(k_t[rows_of(h)], self.d_s[ball, h]) * SCALE)
        self.put(1, ball, h, dot(q_t[rows_of(h)], self.d_s[ball, h], 1, 1) * LN2)

    def finish(self, ball):
        values, inv_rms, normed = self.rows.pop(ball)
        d_out, d_qkv_t = self.d_out.pop(ball), self.d_qkv_t[ball]
        self.sums[: 3 * D, :] += dot(d_qkv_t, normed)
        self.sums[3 * D : 4 * D, :] += dot(self.att_ref[ball], d_out)
        d_normed = dot(self.w_ref[...], d_qkv_t).T
        unit = values * inv_rms
        self.sums[4 * D : 4 * D + 1, :] += jnp.sum(d_normed * unit, axis=0, keepdims=True)
        d_unit = d_normed * self.gain_ref[...]
        along = jnp.mean(d_unit * unit, axis=-1, keepdims=True)
        return d_out.astype(f32) + inv_rms * (d_unit - unit * along)


def normalise(values, gain_ref):
    inv_rms = inverse_rms(values)
    return inv_rms, (values * inv_rms * gain_ref[...]).astype(bf16)


def for_rows(count, copy_row):
    def step(i, carry):
        for j in range(UNROLL):
            copy_row(i * UNROLL + j)
        return carry

    lax.fori_loop(0, count // UNROLL, step, 0)


def gather_chunk(i, order_ref, from_ref, to_ref):
    for r in range(i * CHUNK, (i + 1) * CHUNK):
        to_ref[pl.ds(r, 1), :] = from_ref[pl.ds(order_ref[r], 1), :]


def scatter_chunk(i, order_ref, from_ref, to_ref):
    for r in range(i * CHUNK, (i + 1) * CHUNK):
        to_ref[pl.ds(order_ref[r], 1), :] = from_ref[pl.ds(r, 1), :]


def gather(order_ref, from_ref, to_ref):
    def copy_row(r):
        to_ref[pl.ds(r, 1), :] = from_ref[pl.ds(order_ref[r], 1), :]

    for_rows(to_ref.shape[0], copy_row)


def scatter(order_ref, from_ref, to_ref):
    def copy_row(r):
        to_ref[pl.ds(order_ref[r], 1), :] = from_ref[pl.ds(r, 1), :]

    for_rows(from_ref.shape[0], copy_row)


def arranged(sums):
    gain = sums[4 * D : 4 * D + 16, :]
    parts = [sums[0:D, :].T, sums[D : 2 * D, :].T, gain, sums[2 * D : 3 * D, :].T, sums[3 * D : 4 * D, :], gain]
    return jnp.concatenate(parts, axis=0)


def share(core_ref, sums, halves, mine_ref, other_ref):
    halves[...] = arranged(sums)
    core = core_ref[0]
    mine_ref[...] = halves[pl.ds(pl.multiple_of(core * GRAD_HALF, 16), GRAD_HALF), :]
    other_ref[...] = halves[pl.ds(pl.multiple_of((1 - core) * GRAD_HALF, 16), GRAD_HALF), :].astype(bf16)


def first_kernel(order_ref, x_ref, gain_ref, w_ref, proj_ref, sent_ref, inv_ref, e_out, kept_out, v_out, wt, out, sent, e_s, kept, v_s, att_s, sems):
    balls = e_s.shape[0]
    heads = balls * HEADS
    wt[...] = w_ref[...].T
    forward = Forward(e_s, inv_ref, att_s)
    values, copies = {}, []

    def prepare(ball):
        values[ball] = x_ref[ball_rows(ball), :].astype(f32)
        _, normed = normalise(values[ball], gain_ref)
        parts = project(normed, w_ref, wt)
        forward.parts[ball] = parts
        kept[ball, D : 2 * D, :] = parts[0]
        kept[ball, 2 * D :, :] = parts[1]
        v_s[ball] = parts[4]

    def finish(ball):
        att_t = att_s[ball]
        kept[ball, :D, :] = att_t
        out[ball_rows(ball), :] = values.pop(ball) + dot(att_t, proj_ref[...], 0, 0)
        for n, (source, target) in enumerate(((e_s, e_out), (kept, kept_out), (v_s, v_out))):
            copy = pltpu.make_async_copy(source.at[ball], target.at[ball], sems.at[n, ball])
            copy.start()
            copies.append(copy)

    staggered(
        heads,
        (0, at_first(prepare)),
        (2, forward.score),
        (6, forward.soften),
        (8, forward.attend),
        (8, at_last(finish)),
    )
    gather(order_ref, out, sent)
    sent_ref[...] = sent[...].astype(bf16)
    for copy in copies:
        copy.wait()


def second_kernel(core_ref, order_ref, came_ref, d_out_ref, gain_ref, w_ref, proj_ref, sent_ref, mine_ref, other_ref, wt, came, placed, e_s, inv_s, att_s, d_s, d_qkv_t, d_in, d_came, sums, halves):
    balls = e_s.shape[0]
    wt[...] = w_ref[...].T
    came[...] = came_ref[...].astype(f32)
    sums[...] = jnp.zeros_like(sums)
    forward = Forward(e_s, inv_s, att_s)
    backward = Backward(e_s, inv_s, att_s, d_s, d_qkv_t, w_ref, proj_ref, gain_ref, sums)

    def prepare(ball):
        values = placed[ball_rows(ball), :]
        inv_rms, normed = normalise(values, gain_ref)
        parts = project(normed, w_ref, wt)
        forward.parts[ball] = parts
        backward.parts[ball] = (parts[0], parts[1], parts[4])
        backward.rows[ball] = (values, inv_rms, normed)

    def join(ball):
        backward.join(ball, d_out_ref[ball_rows(ball), :])

    def finish(ball):
        d_in[ball_rows(ball), :] = backward.finish(ball)

    staggered(
        balls * HEADS,
        (0, lambda i: gather_chunk(i, order_ref, came, placed)),
        (8, at_first(prepare)),
        (10, forward.score),
        (14, forward.soften),
        (16, forward.attend),
        (16, at_last(join)),
        (25, backward.weigh),
        (28, backward.score),
        (28, backward.value),
        (30, backward.query_key),
        (30, at_last(finish)),
        (39, lambda i: scatter_chunk(i, order_ref, d_in, d_came)),
    )
    sent_ref[...] = d_came[...].astype(bf16)
    share(core_ref, sums, halves, mine_ref, other_ref)


def third_kernel(core_ref, order_ref, came_ref, x_ref, gain_ref, w_ref, proj_ref, inv_ref, e_in, kept_in, v_in, d_x_ref, mine_ref, other_ref, came, d_first, e_s, kept, v_s, d_s, d_qkv_t, sums, halves, sems):
    balls = e_s.shape[0]
    copies = {}
    for ball in range(balls):
        for n, (source, target) in enumerate(((e_in, e_s), (kept_in, kept), (v_in, v_s))):
            copies[ball, n] = pltpu.make_async_copy(source.at[ball], target.at[ball], sems.at[n, ball])
            if ball < AHEAD:
                copies[ball, n].start()
    came[...] = came_ref[...].astype(f32)
    sums[...] = jnp.zeros_like(sums)
    scatter(order_ref, came, d_first)
    backward = Backward(e_s, inv_ref, kept.at[:, :D, :], d_s, d_qkv_t, w_ref, proj_ref, gain_ref, sums)

    def prepare(ball):
        for n in range(3):
            copies[ball, n].wait()
            if ball + AHEAD < balls:
                copies[ball + AHEAD, n].start()
        values = x_ref[ball_rows(ball), :].astype(f32)
        inv_rms, normed = normalise(values, gain_ref)
        backward.rows[ball] = (values, inv_rms, normed)
        backward.parts[ball] = (kept[ball, D : 2 * D, :], kept[ball, 2 * D :, :], v_s[ball])
        backward.join(ball, d_first[ball_rows(ball), :].astype(bf16))

    def finish(ball):
        d_x_ref[ball_rows(ball), :] = backward.finish(ball).astype(bf16)

    staggered(
        balls * HEADS,
        (0, at_first(prepare)),
        (2, backward.weigh),
        (5, backward.score),
        (5, backward.value),
        (7, backward.query_key),
        (7, at_last(finish)),
    )
    share(core_ref, sums, halves, mine_ref, other_ref)


def last_kernel(core_ref, mine_a, came_a, mine_b, came_b, *refs):
    outs, parts, sems = refs[:6], refs[6:10], refs[10]
    copies = [pltpu.make_async_copy(ref, part, sems.at[n]) for n, (ref, part) in enumerate(zip((mine_a, came_a, mine_b, came_b), parts))]
    for copy in copies:
        copy.start()
    first = core_ref[0] == 0
    for n in range(2):
        gain_ref, qkv_ref, proj_ref = outs[3 * n : 3 * n + 3]
        copies[2 * n].wait()
        copies[2 * n + 1].wait()
        mine, came = parts[2 * n][...].astype(f32), parts[2 * n + 1][...].astype(f32)
        low = jnp.where(first, mine, came)
        high = jnp.where(first, came, mine)
        qkv_ref[:, :D] = low[:D]
        qkv_ref[:, D : 2 * D] = low[D : 2 * D]
        gain_ref[...] = low[2 * D : 2 * D + 1]
        qkv_ref[:, 2 * D :] = high[:D]
        proj_ref[...] = high[D : 2 * D]


SCALARS = pl.BlockSpec(memory_space=pltpu.SMEM)
VECTORS = pl.BlockSpec(memory_space=pltpu.VMEM)
REMAIN = pl.BlockSpec(memory_space=pl.ANY)


def call(kernel, in_specs, outs, scratch):
    return pl.pallas_call(
        kernel,
        in_specs=in_specs,
        out_specs=[spec for spec, _, _ in outs],
        out_shape=[jax.ShapeDtypeStruct(shape, kind) for _, shape, kind in outs],
        scratch_shapes=scratch,
        compiler_params=pltpu.CompilerParams(vmem_limit_bytes=VMEM_LIMIT),
    )


def first_call(order, x, gain, w, proj):
    rows = x.shape[0]
    balls = rows // BALL
    kept = [((balls, HEADS, BALL, BALL), bf16), ((balls, 3 * D, BALL), bf16), ((balls, BALL, D), bf16)]
    return call(
        first_kernel,
        [SCALARS] + [VECTORS] * 4,
        [(VECTORS, (rows, D), bf16), (VECTORS, (balls, HEADS, BALL), f32)]
        + [(REMAIN, shape, kind) for shape, kind in kept],
        [pltpu.VMEM((3 * D, D), bf16), pltpu.VMEM((rows, D), f32), pltpu.VMEM((rows, D), f32)]
        + [pltpu.VMEM(shape, kind) for shape, kind in kept]
        + [pltpu.VMEM((balls, D, BALL), bf16), pltpu.SemaphoreType.DMA((3, balls))],
    )(order, x, gain, w, proj)


def second_call(core, order, came, d_out, gain, w, proj):
    rows = came.shape[0]
    balls = rows // BALL
    weights = pltpu.VMEM((balls, HEADS, BALL, BALL), bf16)
    return call(
        second_kernel,
        [SCALARS] * 2 + [VECTORS] * 5,
        [(VECTORS, (rows, D), bf16), (VECTORS, (GRAD_HALF, D), f32), (VECTORS, (GRAD_HALF, D), bf16)],
        [
            pltpu.VMEM((3 * D, D), bf16),
            pltpu.VMEM((rows, D), f32),
            pltpu.VMEM((rows, D), f32),
            weights,
            pltpu.VMEM((balls, HEADS, BALL), f32),
            pltpu.VMEM((balls, D, BALL), bf16),
            weights,
            pltpu.VMEM((balls, 3 * D, BALL), bf16),
            pltpu.VMEM((rows, D), f32),
            pltpu.VMEM((rows, D), f32),
            pltpu.VMEM((4 * D + 16, D), f32),
            pltpu.VMEM((2 * GRAD_HALF, D), f32),
        ],
    )(core, order, came, d_out, gain, w, proj)


def third_call(core, order, came, x, gain, w, proj, inv, kept):
    rows = came.shape[0]
    balls = rows // BALL
    weights = pltpu.VMEM((balls, HEADS, BALL, BALL), bf16)
    return call(
        third_kernel,
        [SCALARS] * 2 + [VECTORS] * 6 + [REMAIN] * 3,
        [(VECTORS, (rows, D), bf16), (VECTORS, (GRAD_HALF, D), f32), (VECTORS, (GRAD_HALF, D), bf16)],
        [pltpu.VMEM((rows, D), f32), pltpu.VMEM((rows, D), f32)]
        + [pltpu.VMEM(part.shape, part.dtype) for part in kept]
        + [
            weights,
            pltpu.VMEM((balls, 3 * D, BALL), bf16),
            pltpu.VMEM((4 * D + 16, D), f32),
            pltpu.VMEM((2 * GRAD_HALF, D), f32),
            pltpu.SemaphoreType.DMA((3, balls)),
        ],
    )(core, order, came, x, gain, w, proj, inv, *kept)


def last_call(core, *parts):
    shapes = [(1, D), (D, 3 * D), (D, D)] * 2
    return call(
        last_kernel,
        [SCALARS] + [REMAIN] * 4,
        [(VECTORS, shape, f32) for shape in shapes],
        [pltpu.VMEM((GRAD_HALF, D), bf16)] * 4 + [pltpu.SemaphoreType.DMA((4,))],
    )(core, *parts)


def exchange(rows):
    return lax.all_to_all(rows, "wide", split_axis=0, concat_axis=0, tiled=True)


def swap(part, peers, apart):
    return lax.ppermute(part, "wide", [(i, i ^ apart) for i in range(peers)])


def sum_cores(mine, other):
    return mine + swap(other, lax.axis_size("wide"), 1).astype(f32)


def sum_chips(total, apart, until):
    while apart < until:
        part = total.astype(bf16)
        total = part.astype(f32) + swap(part, lax.axis_size("wide"), apart).astype(f32)
        apart *= 2
    return total


def both_halves(total):
    part = total.astype(bf16)
    return part, swap(part, lax.axis_size("wide"), 1)


def body(tokens, cotangent, order_send, order_recv, gain_a, qkv_a, proj_a, gain_b, qkv_b, proj_b):
    core = (lax.axis_index("wide") % 2).astype(jnp.int32).reshape(1)
    gain_a = gain_a.reshape(1, D)
    gain_b = gain_b.reshape(1, D)
    sent, inv, *kept = first_call(order_send, tokens, gain_a, qkv_a, proj_a)
    d_sent, *grads_b = second_call(core, order_recv, exchange(sent), cotangent, gain_b, qkv_b, proj_b)
    came = exchange(d_sent)
    peers = lax.axis_size("wide")
    total_b = sum_chips(sum_cores(*grads_b), 2, peers // 2)
    came, total_b = lax.optimization_barrier((came, total_b))
    total_b = sum_chips(total_b, peers // 2, peers)
    d_tokens, *grads_a = third_call(core, order_send, came, tokens, gain_a, qkv_a, proj_a, inv, kept)
    grads_a, total_b = lax.optimization_barrier((grads_a, total_b))
    sums_b = both_halves(total_b)
    sums_a = both_halves(sum_chips(sum_cores(*grads_a), 2, peers))
    sums = last_call(core, *sums_a, *sums_b)
    d_gain_a, d_qkv_a, d_proj_a, d_gain_b, d_qkv_b, d_proj_b = sums
    return d_tokens, d_gain_a.reshape(D), d_qkv_a, d_proj_a, d_gain_b.reshape(D), d_qkv_b, d_proj_b


def solution(mesh):
    rows = P(("grp", "wide"), None)
    order = P(("grp", "wide"))
    return jax.shard_map(
        body,
        mesh=mesh,
        in_specs=(rows, rows, order, order) + (P(),) * 6,
        out_specs=(rows,) + (P("grp"), P("grp", None), P("grp", None)) * 2,
        check_vma=False,
    )
```

```python
import jax
import jax.numpy as jnp
from jax import lax
from jax.experimental import pallas as pl
from jax.experimental.pallas import tpu as pltpu
from jax.sharding import PartitionSpec as P

D = 128
HEADS = 8
BALL = 256
HEAD_DIM = 16
EPS = 1e-06
LOG2E = 1.4426950408889634
LN2 = 0.6931471805599453
SCALE = HEAD_DIM ** (-0.5)
VMEM_LIMIT = 56 * 1024 * 1024
SMALL_LIMIT = 16 * 1024 * 1024
UNROLL = 128
AHEAD = 3
CHUNK = BALL // HEADS
GRAD_HALF = 2 * D + 16

f32 = jnp.float32
bf16 = jnp.bfloat16


def dot(a, b, ca=1, cb=0):
    return lax.dot_general(a, b, (((ca,), (cb,)), ((), ())), preferred_element_type=f32)


def head_mask(h):
    lane = lax.broadcasted_iota(jnp.int32, (1, D), 1)
    return jnp.where(lane // HEAD_DIM == h, 1.0, 0.0).astype(bf16)


def rows_of(h):
    return slice(h * HEAD_DIM, (h + 1) * HEAD_DIM)


def inverse_rms(values):
    return lax.rsqrt(jnp.mean(values * values, axis=-1, keepdims=True) + EPS)


def staggered(count, *stages):
    last = max(lag for lag, _ in stages)
    for step in range(count + last):
        for lag, stage in stages:
            if 0 <= step - lag < count:
                stage(step - lag)


def at_first(stage):
    return lambda i: stage(i // HEADS) if i % HEADS == 0 else None


def at_last(stage):
    return lambda i: stage(i // HEADS) if i % HEADS == HEADS - 1 else None


def ball_rows(ball):
    return slice(ball * BALL, (ball + 1) * BALL)


def project(normed, w_ref, wt_ref):
    qkv_t = dot(wt_ref[...], normed, 1, 1)
    q_t = (qkv_t[:D] * (SCALE * LOG2E)).astype(bf16)
    k_t = qkv_t[D : 2 * D].astype(bf16)
    v_t = qkv_t[2 * D :].astype(bf16)
    kv = dot(normed, w_ref[:, D:]).astype(bf16)
    return q_t, k_t, v_t, kv[:, :D], kv[:, D:]


class Forward:
    def __init__(self, e_ref, inv_ref, att_ref):
        self.e_ref, self.inv_ref, self.att_ref = e_ref, inv_ref, att_ref
        self.parts, self.scores = {}, {}

    def score(self, i):
        ball, h = divmod(i, HEADS)
        q_t, _, _, k_rows, _ = self.parts[ball]
        self.scores[i] = dot(k_rows * head_mask(h), q_t)

    def soften(self, i):
        ball, h = divmod(i, HEADS)
        own = self.scores.pop(i)
        self.e_ref[ball, h] = jnp.exp2(own - jnp.max(own, axis=0, keepdims=True)).astype(bf16)

    def attend(self, i):
        ball, h = divmod(i, HEADS)
        ones = jnp.ones((HEAD_DIM, BALL), bf16)
        stacked = jnp.concatenate([self.parts[ball][2][rows_of(h)], ones], axis=0)
        summed = dot(stacked, self.e_ref[ball, h])
        inv = 1.0 / summed[HEAD_DIM : HEAD_DIM + 1]
        self.inv_ref[ball, h : h + 1, :] = inv
        self.att_ref[ball, rows_of(h), :] = (summed[:HEAD_DIM] * inv).astype(bf16)


class Backward:
    def __init__(self, e_ref, inv_ref, att_ref, d_s, d_qkv_t, w_ref, proj_ref, gain_ref, sums):
        self.e_ref, self.inv_ref, self.att_ref, self.d_s, self.d_qkv_t = e_ref, inv_ref, att_ref, d_s, d_qkv_t
        self.w_ref, self.proj_ref, self.gain_ref, self.sums = w_ref, proj_ref, gain_ref, sums
        self.parts, self.rows, self.d_out, self.d_att, self.d_weights = {}, {}, {}, {}, {}

    def join(self, ball, d_out):
        inv = [jnp.broadcast_to(self.inv_ref[ball, h : h + 1, :], (HEAD_DIM, BALL)) for h in range(HEADS)]
        self.d_out[ball] = d_out
        self.d_att[ball] = (dot(self.proj_ref[...], d_out, 1, 1) * jnp.concatenate(inv, axis=0)).astype(bf16)

    def weigh(self, i):
        ball, h = divmod(i, HEADS)
        self.d_weights[i] = dot(self.parts[ball][2] * head_mask(h), self.d_att[ball])

    def score(self, i):
        ball, h = divmod(i, HEADS)
        own = self.d_att[ball][rows_of(h)]
        att = self.att_ref[ball, rows_of(h), :]
        delta = jnp.sum(own.astype(f32) * att.astype(f32), axis=0, keepdims=True)
        self.d_s[ball, h] = (self.e_ref[ball, h].astype(f32) * (self.d_weights.pop(i) - delta)).astype(bf16)

    def put(self, part, ball, h, value):
        start = part * D + h * HEAD_DIM
        self.d_qkv_t[ball, start : start + HEAD_DIM, :] = value.astype(bf16)

    def value(self, i):
        ball, h = divmod(i, HEADS)
        self.put(2, ball, h, dot(self.d_att[ball][rows_of(h)], self.e_ref[ball, h], 1, 1))

    def query_key(self, i):
        ball, h = divmod(i, HEADS)
        q_t, k_t, _ = self.parts[ball]
        self.put(0, ball, h, dot(k_t[rows_of(h)], self.d_s[ball, h]) * SCALE)
        self.put(1, ball, h, dot(q_t[rows_of(h)], self.d_s[ball, h], 1, 1) * LN2)

    def finish(self, ball):
        values, inv_rms, normed = self.rows.pop(ball)
        d_out, d_qkv_t = self.d_out.pop(ball), self.d_qkv_t[ball]
        self.sums[: 3 * D, :] += dot(d_qkv_t, normed)
        self.sums[3 * D : 4 * D, :] += dot(self.att_ref[ball], d_out)
        d_normed = dot(self.w_ref[...], d_qkv_t).T
        unit = values * inv_rms
        self.sums[4 * D : 4 * D + 1, :] += jnp.sum(d_normed * unit, axis=0, keepdims=True)
        d_unit = d_normed * self.gain_ref[...]
        along = jnp.mean(d_unit * unit, axis=-1, keepdims=True)
        return d_out.astype(f32) + inv_rms * (d_unit - unit * along)


def normalise(values, gain_ref):
    inv_rms = inverse_rms(values)
    return inv_rms, (values * inv_rms * gain_ref[...]).astype(bf16)


def for_rows(count, copy_row):
    def step(i, carry):
        for j in range(UNROLL):
            copy_row(i * UNROLL + j)
        return carry

    lax.fori_loop(0, count // UNROLL, step, 0)


def gather_chunk(i, order_ref, from_ref, to_ref):
    for r in range(i * CHUNK, (i + 1) * CHUNK):
        to_ref[pl.ds(r, 1), :] = from_ref[pl.ds(order_ref[r], 1), :]


def scatter_chunk(i, order_ref, from_ref, to_ref):
    for r in range(i * CHUNK, (i + 1) * CHUNK):
        to_ref[pl.ds(order_ref[r], 1), :] = from_ref[pl.ds(r, 1), :]


def gather(order_ref, from_ref, to_ref):
    def copy_row(r):
        to_ref[pl.ds(r, 1), :] = from_ref[pl.ds(order_ref[r], 1), :]

    for_rows(to_ref.shape[0], copy_row)


def scatter(order_ref, from_ref, to_ref):
    def copy_row(r):
        to_ref[pl.ds(order_ref[r], 1), :] = from_ref[pl.ds(r, 1), :]

    for_rows(from_ref.shape[0], copy_row)


def arranged(sums):
    gain = sums[4 * D : 4 * D + 16, :]
    parts = [sums[0:D, :].T, sums[D : 2 * D, :].T, gain, sums[2 * D : 3 * D, :].T, sums[3 * D : 4 * D, :], gain]
    return jnp.concatenate(parts, axis=0)


def share(core_ref, sums, halves, mine_ref, other_ref):
    halves[...] = arranged(sums)
    core = core_ref[0]
    mine_ref[...] = halves[pl.ds(pl.multiple_of(core * GRAD_HALF, 16), GRAD_HALF), :]
    other_ref[...] = halves[pl.ds(pl.multiple_of((1 - core) * GRAD_HALF, 16), GRAD_HALF), :].astype(bf16)


def first_kernel(order_ref, x_ref, gain_ref, w_ref, proj_ref, sent_ref, inv_ref, e_out, kept_out, v_out, wt, out, sent, e_s, kept, v_s, att_s, sems):
    balls = e_s.shape[0]
    heads = balls * HEADS
    wt[...] = w_ref[...].T
    forward = Forward(e_s, inv_ref, att_s)
    values, copies = {}, []

    def prepare(ball):
        values[ball] = x_ref[ball_rows(ball), :].astype(f32)
        _, normed = normalise(values[ball], gain_ref)
        parts = project(normed, w_ref, wt)
        forward.parts[ball] = parts
        kept[ball, D : 2 * D, :] = parts[0]
        kept[ball, 2 * D :, :] = parts[1]
        v_s[ball] = parts[4]

    def finish(ball):
        att_t = att_s[ball]
        kept[ball, :D, :] = att_t
        out[ball_rows(ball), :] = values.pop(ball) + dot(att_t, proj_ref[...], 0, 0)
        for n, (source, target) in enumerate(((e_s, e_out), (kept, kept_out), (v_s, v_out))):
            copy = pltpu.make_async_copy(source.at[ball], target.at[ball], sems.at[n, ball])
            copy.start()
            copies.append(copy)

    staggered(
        heads,
        (0, at_first(prepare)),
        (3, forward.score),
        (6, forward.soften),
        (9, forward.attend),
        (13, at_last(finish)),
    )
    gather(order_ref, out, sent)
    sent_ref[...] = sent[...].astype(bf16)
    for copy in copies:
        copy.wait()


def second_kernel(core_ref, order_ref, came_ref, d_out_ref, gain_ref, w_ref, proj_ref, sent_ref, mine_ref, other_ref, wt, came, placed, e_s, inv_s, att_s, d_s, d_qkv_t, d_in, d_came, sums, halves):
    balls = e_s.shape[0]
    wt[...] = w_ref[...].T
    came[...] = came_ref[...].astype(f32)
    sums[...] = jnp.zeros_like(sums)
    forward = Forward(e_s, inv_s, att_s)
    backward = Backward(e_s, inv_s, att_s, d_s, d_qkv_t, w_ref, proj_ref, gain_ref, sums)

    def prepare(ball):
        values = placed[ball_rows(ball), :]
        inv_rms, normed = normalise(values, gain_ref)
        parts = project(normed, w_ref, wt)
        forward.parts[ball] = parts
        backward.parts[ball] = (parts[0], parts[1], parts[4])
        backward.rows[ball] = (values, inv_rms, normed)

    def join(ball):
        backward.join(ball, d_out_ref[ball_rows(ball), :])

    def finish(ball):
        d_in[ball_rows(ball), :] = backward.finish(ball)

    staggered(
        balls * HEADS,
        (0, lambda i: gather_chunk(i, order_ref, came, placed)),
        (8, at_first(prepare)),
        (10, forward.score),
        (14, forward.soften),
        (16, forward.attend),
        (16, at_last(join)),
        (25, backward.value),
        (25, backward.weigh),
        (27, backward.score),
        (29, backward.query_key),
        (31, at_last(finish)),
        (41, lambda i: scatter_chunk(i, order_ref, d_in, d_came)),
    )
    sent_ref[...] = d_came[...].astype(bf16)
    share(core_ref, sums, halves, mine_ref, other_ref)


def third_kernel(core_ref, order_ref, came_ref, x_ref, gain_ref, w_ref, proj_ref, inv_ref, e_in, kept_in, v_in, d_x_ref, mine_ref, other_ref, came, d_first, e_s, kept, v_s, d_s, d_qkv_t, sums, halves, sems):
    balls = e_s.shape[0]
    copies = {}
    for ball in range(balls):
        for n, (source, target) in enumerate(((e_in, e_s), (kept_in, kept), (v_in, v_s))):
            copies[ball, n] = pltpu.make_async_copy(source.at[ball], target.at[ball], sems.at[n, ball])
            if ball < AHEAD:
                copies[ball, n].start()
    came[...] = came_ref[...].astype(f32)
    sums[...] = jnp.zeros_like(sums)
    scatter(order_ref, came, d_first)
    backward = Backward(e_s, inv_ref, kept.at[:, :D, :], d_s, d_qkv_t, w_ref, proj_ref, gain_ref, sums)

    def prepare(ball):
        for n in range(3):
            copies[ball, n].wait()
            if ball + AHEAD < balls:
                copies[ball + AHEAD, n].start()
        values = x_ref[ball_rows(ball), :].astype(f32)
        inv_rms, normed = normalise(values, gain_ref)
        backward.rows[ball] = (values, inv_rms, normed)
        backward.parts[ball] = (kept[ball, D : 2 * D, :], kept[ball, 2 * D :, :], v_s[ball])
        backward.join(ball, d_first[ball_rows(ball), :].astype(bf16))

    def finish(ball):
        d_x_ref[ball_rows(ball), :] = backward.finish(ball).astype(bf16)

    staggered(
        balls * HEADS,
        (0, at_first(prepare)),
        (4, backward.value),
        (4, backward.weigh),
        (7, backward.score),
        (10, backward.query_key),
        (13, at_last(finish)),
    )
    share(core_ref, sums, halves, mine_ref, other_ref)


def last_kernel(core_ref, mine_a, came_a, mine_b, came_b, *refs):
    outs, parts, sems = refs[:6], refs[6:10], refs[10]
    copies = [pltpu.make_async_copy(ref, part, sems.at[n]) for n, (ref, part) in enumerate(zip((mine_a, came_a, mine_b, came_b), parts))]
    for copy in copies:
        copy.start()
    first = core_ref[0] == 0
    for n in range(2):
        gain_ref, qkv_ref, proj_ref = outs[3 * n : 3 * n + 3]
        copies[2 * n].wait()
        copies[2 * n + 1].wait()
        mine, came = parts[2 * n][...].astype(f32), parts[2 * n + 1][...].astype(f32)
        low = jnp.where(first, mine, came)
        high = jnp.where(first, came, mine)
        qkv_ref[:, :D] = low[:D]
        qkv_ref[:, D : 2 * D] = low[D : 2 * D]
        gain_ref[...] = low[2 * D : 2 * D + 1]
        qkv_ref[:, 2 * D :] = high[:D]
        proj_ref[...] = high[D : 2 * D]


SCALARS = pl.BlockSpec(memory_space=pltpu.SMEM)
VECTORS = pl.BlockSpec(memory_space=pltpu.VMEM)
REMAIN = pl.BlockSpec(memory_space=pl.ANY)


def call(kernel, in_specs, outs, scratch, limit=VMEM_LIMIT):
    return pl.pallas_call(
        kernel,
        in_specs=in_specs,
        out_specs=[spec for spec, _, _ in outs],
        out_shape=[jax.ShapeDtypeStruct(shape, kind) for _, shape, kind in outs],
        scratch_shapes=scratch,
        compiler_params=pltpu.CompilerParams(vmem_limit_bytes=limit),
    )


def first_call(order, x, gain, w, proj):
    rows = x.shape[0]
    balls = rows // BALL
    kept = [((balls, HEADS, BALL, BALL), bf16), ((balls, 3 * D, BALL), bf16), ((balls, BALL, D), bf16)]
    return call(
        first_kernel,
        [SCALARS] + [VECTORS] * 4,
        [(VECTORS, (rows, D), bf16), (VECTORS, (balls, HEADS, BALL), f32)]
        + [(REMAIN, shape, kind) for shape, kind in kept],
        [pltpu.VMEM((3 * D, D), bf16), pltpu.VMEM((rows, D), f32), pltpu.VMEM((rows, D), f32)]
        + [pltpu.VMEM(shape, kind) for shape, kind in kept]
        + [pltpu.VMEM((balls, D, BALL), bf16), pltpu.SemaphoreType.DMA((3, balls))],
    )(order, x, gain, w, proj)


def second_call(core, order, came, d_out, gain, w, proj):
    rows = came.shape[0]
    balls = rows // BALL
    weights = pltpu.VMEM((balls, HEADS, BALL, BALL), bf16)
    return call(
        second_kernel,
        [SCALARS] * 2 + [VECTORS] * 5,
        [(VECTORS, (rows, D), bf16), (VECTORS, (GRAD_HALF, D), f32), (VECTORS, (GRAD_HALF, D), bf16)],
        [
            pltpu.VMEM((3 * D, D), bf16),
            pltpu.VMEM((rows, D), f32),
            pltpu.VMEM((rows, D), f32),
            weights,
            pltpu.VMEM((balls, HEADS, BALL), f32),
            pltpu.VMEM((balls, D, BALL), bf16),
            weights,
            pltpu.VMEM((balls, 3 * D, BALL), bf16),
            pltpu.VMEM((rows, D), f32),
            pltpu.VMEM((rows, D), f32),
            pltpu.VMEM((4 * D + 16, D), f32),
            pltpu.VMEM((2 * GRAD_HALF, D), f32),
        ],
    )(core, order, came, d_out, gain, w, proj)


def third_call(core, order, came, x, gain, w, proj, inv, kept):
    rows = came.shape[0]
    balls = rows // BALL
    weights = pltpu.VMEM((balls, HEADS, BALL, BALL), bf16)
    return call(
        third_kernel,
        [SCALARS] * 2 + [VECTORS] * 6 + [REMAIN] * 3,
        [(VECTORS, (rows, D), bf16), (VECTORS, (GRAD_HALF, D), f32), (VECTORS, (GRAD_HALF, D), bf16)],
        [pltpu.VMEM((rows, D), f32), pltpu.VMEM((rows, D), f32)]
        + [pltpu.VMEM(part.shape, part.dtype) for part in kept]
        + [
            weights,
            pltpu.VMEM((balls, 3 * D, BALL), bf16),
            pltpu.VMEM((4 * D + 16, D), f32),
            pltpu.VMEM((2 * GRAD_HALF, D), f32),
            pltpu.SemaphoreType.DMA((3, balls)),
        ],
    )(core, order, came, x, gain, w, proj, inv, *kept)


def last_call(core, *parts):
    shapes = [(1, D), (D, 3 * D), (D, D)] * 2
    return call(
        last_kernel,
        [SCALARS] + [REMAIN] * 4,
        [(VECTORS, shape, f32) for shape in shapes],
        [pltpu.VMEM((GRAD_HALF, D), bf16)] * 4 + [pltpu.SemaphoreType.DMA((4,))],
        SMALL_LIMIT,
    )(core, *parts)


def exchange(rows):
    return lax.all_to_all(rows, "wide", split_axis=0, concat_axis=0, tiled=True)


def swap(part, peers, apart):
    return lax.ppermute(part, "wide", [(i, i ^ apart) for i in range(peers)])


def sum_cores(mine, other):
    return mine + swap(other, lax.axis_size("wide"), 1).astype(f32)


def sum_chips(total, apart, until):
    while apart < until:
        part = total.astype(bf16)
        total = part.astype(f32) + swap(part, lax.axis_size("wide"), apart).astype(f32)
        apart *= 2
    return total


def both_halves(total):
    part = total.astype(bf16)
    return part, swap(part, lax.axis_size("wide"), 1)


def body(tokens, cotangent, order_send, order_recv, gain_a, qkv_a, proj_a, gain_b, qkv_b, proj_b):
    core = (lax.axis_index("wide") % 2).astype(jnp.int32).reshape(1)
    order_send, core = lax.optimization_barrier((order_send, core))
    gain_a = gain_a.reshape(1, D)
    gain_b = gain_b.reshape(1, D)
    sent, inv, *kept = first_call(order_send, tokens, gain_a, qkv_a, proj_a)
    d_sent, *grads_b = second_call(core, order_recv, exchange(sent), cotangent, gain_b, qkv_b, proj_b)
    came = exchange(d_sent)
    peers = lax.axis_size("wide")
    total_b = sum_chips(sum_cores(*grads_b), 2, peers // 2)
    came, total_b = lax.optimization_barrier((came, total_b))
    total_b = sum_chips(total_b, peers // 2, peers)
    d_tokens, *grads_a = third_call(core, order_send, came, tokens, gain_a, qkv_a, proj_a, inv, kept)
    grads_a, total_b = lax.optimization_barrier((grads_a, total_b))
    sums_b = both_halves(total_b)
    sums_a = both_halves(sum_chips(sum_cores(*grads_a), 2, peers))
    sums = last_call(core, *sums_a, *sums_b)
    d_gain_a, d_qkv_a, d_proj_a, d_gain_b, d_qkv_b, d_proj_b = sums
    return d_tokens, d_gain_a.reshape(D), d_qkv_a, d_proj_a, d_gain_b.reshape(D), d_qkv_b, d_proj_b


def solution(mesh):
    rows = P(("grp", "wide"), None)
    order = P(("grp", "wide"))
    return jax.shard_map(
        body,
        mesh=mesh,
        in_specs=(rows, rows, order, order) + (P(),) * 6,
        out_specs=(rows,) + (P("grp"), P("grp", None), P("grp", None)) * 2,
        check_vma=False,
    )
```

```python
import jax
import jax.numpy as jnp
from jax import lax
from jax.experimental import pallas as pl
from jax.experimental.pallas import tpu as pltpu
from jax.sharding import PartitionSpec as P

D = 128
HEADS = 8
BALL = 256
HEAD_DIM = 16
EPS = 1e-06
LOG2E = 1.4426950408889634
LN2 = 0.6931471805599453
SCALE = HEAD_DIM ** (-0.5)
VMEM_LIMIT = 56 * 1024 * 1024
SMALL_LIMIT = 16 * 1024 * 1024
UNROLL = 128
AHEAD = 3
CHUNK = BALL // HEADS
GRAD_HALF = 2 * D + 16

f32 = jnp.float32
bf16 = jnp.bfloat16


def dot(a, b, ca=1, cb=0):
    return lax.dot_general(a, b, (((ca,), (cb,)), ((), ())), preferred_element_type=f32)


def head_mask(h):
    lane = lax.broadcasted_iota(jnp.int32, (1, D), 1)
    return jnp.where(lane // HEAD_DIM == h, 1.0, 0.0).astype(bf16)


def rows_of(h):
    return slice(h * HEAD_DIM, (h + 1) * HEAD_DIM)


def inverse_rms(values):
    return lax.rsqrt(jnp.mean(values * values, axis=-1, keepdims=True) + EPS)


def staggered(count, *stages):
    last = max(lag for lag, _ in stages)
    for step in range(count + last):
        for lag, stage in stages:
            if 0 <= step - lag < count:
                stage(step - lag)


def at_first(stage):
    return lambda i: stage(i // HEADS) if i % HEADS == 0 else None


def at_last(stage):
    return lambda i: stage(i // HEADS) if i % HEADS == HEADS - 1 else None


def ball_rows(ball):
    return slice(ball * BALL, (ball + 1) * BALL)


def project(normed, w_ref, wt_ref):
    qkv_t = dot(wt_ref[...], normed, 1, 1)
    q_t = (qkv_t[:D] * (SCALE * LOG2E)).astype(bf16)
    k_t = qkv_t[D : 2 * D].astype(bf16)
    v_t = qkv_t[2 * D :].astype(bf16)
    kv = dot(normed, w_ref[:, D:]).astype(bf16)
    return q_t, k_t, v_t, kv[:, :D], kv[:, D:]


class Forward:
    def __init__(self, e_ref, inv_ref, att_ref):
        self.e_ref, self.inv_ref, self.att_ref = e_ref, inv_ref, att_ref
        self.parts, self.scores = {}, {}

    def score(self, i):
        ball, h = divmod(i, HEADS)
        q_t, _, _, k_rows, _ = self.parts[ball]
        self.scores[i] = dot(k_rows * head_mask(h), q_t)

    def soften(self, i):
        ball, h = divmod(i, HEADS)
        own = self.scores.pop(i)
        self.e_ref[ball, h] = jnp.exp2(own - jnp.max(own, axis=0, keepdims=True)).astype(bf16)

    def attend(self, i):
        ball, h = divmod(i, HEADS)
        ones = jnp.ones((HEAD_DIM, BALL), bf16)
        stacked = jnp.concatenate([self.parts[ball][2][rows_of(h)], ones], axis=0)
        summed = dot(stacked, self.e_ref[ball, h])
        inv = 1.0 / summed[HEAD_DIM : HEAD_DIM + 1]
        self.inv_ref[ball, h : h + 1, :] = inv
        self.att_ref[ball, rows_of(h), :] = (summed[:HEAD_DIM] * inv).astype(bf16)


class Backward:
    def __init__(self, e_ref, inv_ref, att_ref, d_s, d_qkv_t, w_ref, proj_ref, gain_ref, sums):
        self.e_ref, self.inv_ref, self.att_ref, self.d_s, self.d_qkv_t = e_ref, inv_ref, att_ref, d_s, d_qkv_t
        self.w_ref, self.proj_ref, self.gain_ref, self.sums = w_ref, proj_ref, gain_ref, sums
        self.parts, self.rows, self.d_out, self.d_att, self.d_weights = {}, {}, {}, {}, {}

    def join(self, ball, d_out):
        inv = [jnp.broadcast_to(self.inv_ref[ball, h : h + 1, :], (HEAD_DIM, BALL)) for h in range(HEADS)]
        self.d_out[ball] = d_out
        self.d_att[ball] = (dot(self.proj_ref[...], d_out, 1, 1) * jnp.concatenate(inv, axis=0)).astype(bf16)

    def weigh(self, i):
        ball, h = divmod(i, HEADS)
        self.d_weights[i] = dot(self.parts[ball][2] * head_mask(h), self.d_att[ball]).astype(bf16)

    def score(self, i):
        ball, h = divmod(i, HEADS)
        own = self.d_att[ball][rows_of(h)]
        att = self.att_ref[ball, rows_of(h), :]
        delta = jnp.sum(own.astype(f32) * att.astype(f32), axis=0, keepdims=True)
        self.d_s[ball, h] = (self.e_ref[ball, h].astype(f32) * (self.d_weights.pop(i).astype(f32) - delta)).astype(bf16)

    def put(self, part, ball, h, value):
        start = part * D + h * HEAD_DIM
        self.d_qkv_t[ball, start : start + HEAD_DIM, :] = value.astype(bf16)

    def value(self, i):
        ball, h = divmod(i, HEADS)
        self.put(2, ball, h, dot(self.d_att[ball][rows_of(h)], self.e_ref[ball, h], 1, 1))

    def query_key(self, i):
        ball, h = divmod(i, HEADS)
        q_t, k_t, _ = self.parts[ball]
        self.put(0, ball, h, dot(k_t[rows_of(h)], self.d_s[ball, h]) * SCALE)
        self.put(1, ball, h, dot(q_t[rows_of(h)], self.d_s[ball, h], 1, 1) * LN2)

    def finish(self, ball):
        values, inv_rms, normed = self.rows.pop(ball)
        d_out, d_qkv_t = self.d_out.pop(ball), self.d_qkv_t[ball]
        self.sums[: 3 * D, :] += dot(d_qkv_t, normed)
        self.sums[3 * D : 4 * D, :] += dot(self.att_ref[ball], d_out)
        d_normed = dot(self.w_ref[...], d_qkv_t).T
        unit = values * inv_rms
        self.sums[4 * D : 4 * D + 1, :] += jnp.sum(d_normed * unit, axis=0, keepdims=True)
        d_unit = d_normed * self.gain_ref[...]
        along = jnp.mean(d_unit * unit, axis=-1, keepdims=True)
        return d_out.astype(f32) + inv_rms * (d_unit - unit * along)


def normalise(values, gain_ref):
    inv_rms = inverse_rms(values)
    return inv_rms, (values * inv_rms * gain_ref[...]).astype(bf16)


def for_rows(count, copy_row):
    def step(i, carry):
        for j in range(UNROLL):
            copy_row(i * UNROLL + j)
        return carry

    lax.fori_loop(0, count // UNROLL, step, 0)


def gather_chunk(i, order_ref, from_ref, to_ref):
    for r in range(i * CHUNK, (i + 1) * CHUNK):
        to_ref[pl.ds(r, 1), :] = from_ref[pl.ds(order_ref[r], 1), :]


def scatter_chunk(i, order_ref, from_ref, to_ref):
    for r in range(i * CHUNK, (i + 1) * CHUNK):
        to_ref[pl.ds(order_ref[r], 1), :] = from_ref[pl.ds(r, 1), :]


def gather(order_ref, from_ref, to_ref):
    def copy_row(r):
        to_ref[pl.ds(r, 1), :] = from_ref[pl.ds(order_ref[r], 1), :]

    for_rows(to_ref.shape[0], copy_row)


def scatter(order_ref, from_ref, to_ref):
    def copy_row(r):
        to_ref[pl.ds(order_ref[r], 1), :] = from_ref[pl.ds(r, 1), :]

    for_rows(from_ref.shape[0], copy_row)


def arranged(sums):
    gain = sums[4 * D : 4 * D + 16, :]
    parts = [sums[0:D, :].T, sums[D : 2 * D, :].T, gain, sums[2 * D : 3 * D, :].T, sums[3 * D : 4 * D, :], gain]
    return jnp.concatenate(parts, axis=0)


def share(core_ref, sums, halves, mine_ref, other_ref):
    halves[...] = arranged(sums)
    core = core_ref[0]
    mine_ref[...] = halves[pl.ds(pl.multiple_of(core * GRAD_HALF, 16), GRAD_HALF), :]
    other_ref[...] = halves[pl.ds(pl.multiple_of((1 - core) * GRAD_HALF, 16), GRAD_HALF), :].astype(bf16)


def first_kernel(order_ref, x_ref, gain_ref, w_ref, proj_ref, sent_ref, inv_ref, e_out, kept_out, v_out, wt, out, sent, e_s, kept, v_s, att_s, sems):
    balls = e_s.shape[0]
    heads = balls * HEADS
    wt[...] = w_ref[...].T
    forward = Forward(e_s, inv_ref, att_s)
    values, copies = {}, []

    def prepare(ball):
        values[ball] = x_ref[ball_rows(ball), :].astype(f32)
        _, normed = normalise(values[ball], gain_ref)
        parts = project(normed, w_ref, wt)
        forward.parts[ball] = parts
        kept[ball, D : 2 * D, :] = parts[0]
        kept[ball, 2 * D :, :] = parts[1]
        v_s[ball] = parts[4]

    def finish(ball):
        att_t = att_s[ball]
        kept[ball, :D, :] = att_t
        out[ball_rows(ball), :] = values.pop(ball) + dot(att_t, proj_ref[...], 0, 0)
        for n, (source, target) in enumerate(((e_s, e_out), (kept, kept_out), (v_s, v_out))):
            copy = pltpu.make_async_copy(source.at[ball], target.at[ball], sems.at[n, ball])
            copy.start()
            copies.append(copy)

    staggered(
        heads,
        (0, at_first(prepare)),
        (4, forward.score),
        (8, forward.soften),
        (12, forward.attend),
        (17, at_last(finish)),
    )
    gather(order_ref, out, sent)
    sent_ref[...] = sent[...].astype(bf16)
    for copy in copies:
        copy.wait()


def second_kernel(core_ref, order_ref, came_ref, d_out_ref, gain_ref, w_ref, proj_ref, sent_ref, mine_ref, other_ref, wt, came, placed, e_s, inv_s, att_s, d_s, d_qkv_t, d_in, d_came, sums, halves):
    balls = e_s.shape[0]
    wt[...] = w_ref[...].T
    came[...] = came_ref[...].astype(f32)
    sums[...] = jnp.zeros_like(sums)
    forward = Forward(e_s, inv_s, att_s)
    backward = Backward(e_s, inv_s, att_s, d_s, d_qkv_t, w_ref, proj_ref, gain_ref, sums)

    def prepare(ball):
        values = placed[ball_rows(ball), :]
        inv_rms, normed = normalise(values, gain_ref)
        parts = project(normed, w_ref, wt)
        forward.parts[ball] = parts
        backward.parts[ball] = (parts[0], parts[1], parts[4])
        backward.rows[ball] = (values, inv_rms, normed)

    def join(ball):
        backward.join(ball, d_out_ref[ball_rows(ball), :])

    def finish(ball):
        d_in[ball_rows(ball), :] = backward.finish(ball)

    staggered(
        balls * HEADS,
        (0, lambda i: gather_chunk(i, order_ref, came, placed)),
        (8, at_first(prepare)),
        (10, forward.score),
        (14, forward.soften),
        (16, forward.attend),
        (16, at_last(join)),
        (25, backward.value),
        (25, backward.weigh),
        (27, backward.score),
        (29, backward.query_key),
        (31, at_last(finish)),
        (41, lambda i: scatter_chunk(i, order_ref, d_in, d_came)),
    )
    sent_ref[...] = d_came[...].astype(bf16)
    share(core_ref, sums, halves, mine_ref, other_ref)


def third_kernel(core_ref, order_ref, came_ref, x_ref, gain_ref, w_ref, proj_ref, inv_ref, e_in, kept_in, v_in, d_x_ref, mine_ref, other_ref, came, d_first, e_s, kept, v_s, d_s, d_qkv_t, sums, halves, sems):
    balls = e_s.shape[0]
    copies = {}
    for ball in range(balls):
        for n, (source, target) in enumerate(((e_in, e_s), (kept_in, kept), (v_in, v_s))):
            copies[ball, n] = pltpu.make_async_copy(source.at[ball], target.at[ball], sems.at[n, ball])
            if ball < AHEAD:
                copies[ball, n].start()
    came[...] = came_ref[...].astype(f32)
    sums[...] = jnp.zeros_like(sums)
    scatter(order_ref, came, d_first)
    backward = Backward(e_s, inv_ref, kept.at[:, :D, :], d_s, d_qkv_t, w_ref, proj_ref, gain_ref, sums)

    def prepare(ball):
        for n in range(3):
            copies[ball, n].wait()
            if ball + AHEAD < balls:
                copies[ball + AHEAD, n].start()
        values = x_ref[ball_rows(ball), :].astype(f32)
        inv_rms, normed = normalise(values, gain_ref)
        backward.rows[ball] = (values, inv_rms, normed)
        backward.parts[ball] = (kept[ball, D : 2 * D, :], kept[ball, 2 * D :, :], v_s[ball])
        backward.join(ball, d_first[ball_rows(ball), :].astype(bf16))

    def finish(ball):
        d_x_ref[ball_rows(ball), :] = backward.finish(ball).astype(bf16)

    staggered(
        balls * HEADS,
        (0, at_first(prepare)),
        (4, backward.value),
        (4, backward.weigh),
        (7, backward.score),
        (10, backward.query_key),
        (13, at_last(finish)),
    )
    share(core_ref, sums, halves, mine_ref, other_ref)


def last_kernel(core_ref, mine_a, came_a, mine_b, came_b, *refs):
    outs, parts, sems = refs[:6], refs[6:10], refs[10]
    copies = [pltpu.make_async_copy(ref, part, sems.at[n]) for n, (ref, part) in enumerate(zip((mine_a, came_a, mine_b, came_b), parts))]
    for copy in copies:
        copy.start()
    first = core_ref[0] == 0
    for n in range(2):
        gain_ref, qkv_ref, proj_ref = outs[3 * n : 3 * n + 3]
        copies[2 * n].wait()
        copies[2 * n + 1].wait()
        mine, came = parts[2 * n][...].astype(f32), parts[2 * n + 1][...].astype(f32)
        low = jnp.where(first, mine, came)
        high = jnp.where(first, came, mine)
        qkv_ref[:, :D] = low[:D]
        qkv_ref[:, D : 2 * D] = low[D : 2 * D]
        gain_ref[...] = low[2 * D : 2 * D + 1]
        qkv_ref[:, 2 * D :] = high[:D]
        proj_ref[...] = high[D : 2 * D]


SCALARS = pl.BlockSpec(memory_space=pltpu.SMEM)
VECTORS = pl.BlockSpec(memory_space=pltpu.VMEM)
REMAIN = pl.BlockSpec(memory_space=pl.ANY)


def call(kernel, in_specs, outs, scratch, limit=VMEM_LIMIT):
    return pl.pallas_call(
        kernel,
        in_specs=in_specs,
        out_specs=[spec for spec, _, _ in outs],
        out_shape=[jax.ShapeDtypeStruct(shape, kind) for _, shape, kind in outs],
        scratch_shapes=scratch,
        compiler_params=pltpu.CompilerParams(vmem_limit_bytes=limit),
    )


def first_call(order, x, gain, w, proj):
    rows = x.shape[0]
    balls = rows // BALL
    kept = [((balls, HEADS, BALL, BALL), bf16), ((balls, 3 * D, BALL), bf16), ((balls, BALL, D), bf16)]
    return call(
        first_kernel,
        [SCALARS] + [VECTORS] * 4,
        [(VECTORS, (rows, D), bf16), (VECTORS, (balls, HEADS, BALL), f32)]
        + [(REMAIN, shape, kind) for shape, kind in kept],
        [pltpu.VMEM((3 * D, D), bf16), pltpu.VMEM((rows, D), f32), pltpu.VMEM((rows, D), f32)]
        + [pltpu.VMEM(shape, kind) for shape, kind in kept]
        + [pltpu.VMEM((balls, D, BALL), bf16), pltpu.SemaphoreType.DMA((3, balls))],
    )(order, x, gain, w, proj)


def second_call(core, order, came, d_out, gain, w, proj):
    rows = came.shape[0]
    balls = rows // BALL
    weights = pltpu.VMEM((balls, HEADS, BALL, BALL), bf16)
    return call(
        second_kernel,
        [SCALARS] * 2 + [VECTORS] * 5,
        [(VECTORS, (rows, D), bf16), (VECTORS, (GRAD_HALF, D), f32), (VECTORS, (GRAD_HALF, D), bf16)],
        [
            pltpu.VMEM((3 * D, D), bf16),
            pltpu.VMEM((rows, D), f32),
            pltpu.VMEM((rows, D), f32),
            weights,
            pltpu.VMEM((balls, HEADS, BALL), f32),
            pltpu.VMEM((balls, D, BALL), bf16),
            weights,
            pltpu.VMEM((balls, 3 * D, BALL), bf16),
            pltpu.VMEM((rows, D), f32),
            pltpu.VMEM((rows, D), f32),
            pltpu.VMEM((4 * D + 16, D), f32),
            pltpu.VMEM((2 * GRAD_HALF, D), f32),
        ],
    )(core, order, came, d_out, gain, w, proj)


def third_call(core, order, came, x, gain, w, proj, inv, kept):
    rows = came.shape[0]
    balls = rows // BALL
    weights = pltpu.VMEM((balls, HEADS, BALL, BALL), bf16)
    return call(
        third_kernel,
        [SCALARS] * 2 + [VECTORS] * 6 + [REMAIN] * 3,
        [(VECTORS, (rows, D), bf16), (VECTORS, (GRAD_HALF, D), f32), (VECTORS, (GRAD_HALF, D), bf16)],
        [pltpu.VMEM((rows, D), f32), pltpu.VMEM((rows, D), f32)]
        + [pltpu.VMEM(part.shape, part.dtype) for part in kept]
        + [
            weights,
            pltpu.VMEM((balls, 3 * D, BALL), bf16),
            pltpu.VMEM((4 * D + 16, D), f32),
            pltpu.VMEM((2 * GRAD_HALF, D), f32),
            pltpu.SemaphoreType.DMA((3, balls)),
        ],
    )(core, order, came, x, gain, w, proj, inv, *kept)


def last_call(core, *parts):
    shapes = [(1, D), (D, 3 * D), (D, D)] * 2
    return call(
        last_kernel,
        [SCALARS] + [REMAIN] * 4,
        [(VECTORS, shape, f32) for shape in shapes],
        [pltpu.VMEM((GRAD_HALF, D), bf16)] * 4 + [pltpu.SemaphoreType.DMA((4,))],
        SMALL_LIMIT,
    )(core, *parts)


def exchange(rows):
    return lax.all_to_all(rows, "wide", split_axis=0, concat_axis=0, tiled=True)


def swap(part, peers, apart):
    return lax.ppermute(part, "wide", [(i, i ^ apart) for i in range(peers)])


def sum_cores(mine, other):
    return mine + swap(other, lax.axis_size("wide"), 1).astype(f32)


def sum_chips(total, apart, until):
    while apart < until:
        part = total.astype(bf16)
        total = part.astype(f32) + swap(part, lax.axis_size("wide"), apart).astype(f32)
        apart *= 2
    return total


def both_halves(total):
    part = total.astype(bf16)
    return part, swap(part, lax.axis_size("wide"), 1)


def body(tokens, cotangent, order_send, order_recv, gain_a, qkv_a, proj_a, gain_b, qkv_b, proj_b):
    core = (lax.axis_index("wide") % 2).astype(jnp.int32).reshape(1)
    order_send, core = lax.optimization_barrier((order_send, core))
    gain_a = gain_a.reshape(1, D)
    gain_b = gain_b.reshape(1, D)
    sent, inv, *kept = first_call(order_send, tokens, gain_a, qkv_a, proj_a)
    d_sent, *grads_b = second_call(core, order_recv, exchange(sent), cotangent, gain_b, qkv_b, proj_b)
    came = exchange(d_sent)
    peers = lax.axis_size("wide")
    total_b = sum_chips(sum_cores(*grads_b), 2, peers // 2)
    came, total_b = lax.optimization_barrier((came, total_b))
    total_b = sum_chips(total_b, peers // 2, peers)
    d_tokens, *grads_a = third_call(core, order_send, came, tokens, gain_a, qkv_a, proj_a, inv, kept)
    grads_a, total_b = lax.optimization_barrier((grads_a, total_b))
    sums_b = both_halves(total_b)
    sums_a = both_halves(sum_chips(sum_cores(*grads_a), 2, peers))
    sums = last_call(core, *sums_a, *sums_b)
    d_gain_a, d_qkv_a, d_proj_a, d_gain_b, d_qkv_b, d_proj_b = sums
    return d_tokens, d_gain_a.reshape(D), d_qkv_a, d_proj_a, d_gain_b.reshape(D), d_qkv_b, d_proj_b


def solution(mesh):
    rows = P(("grp", "wide"), None)
    order = P(("grp", "wide"))
    return jax.shard_map(
        body,
        mesh=mesh,
        in_specs=(rows, rows, order, order) + (P(),) * 6,
        out_specs=(rows,) + (P("grp"), P("grp", None), P("grp", None)) * 2,
        check_vma=False,
    )
```
